32 devices in a mesh: blk: 2 (over x), table: 16 (over z, y, core).
Axes of the slice: x: 2, y: 2, z: 4, core: 2. Of those that a mesh axis runs over, the one named last changes fastest.
Arguments:
- id_table: bfloat16 [131072, 256], P('table'), may hold values from -6 to 6
- w_first: bfloat16 [256, 4096], replicated, may hold values from -0.375 to 0.375
- w_second: bfloat16 [4096, 256], replicated, may hold values from -0.09375 to 0.09375
- owner_ids: int32 [8192, 8], P(('blk', 'table')), may hold values from 0 to 15, all different within a row; in each aligned block of 256 rows (0 to 255, 256 to 511, ...) at most 192 rows name the same one
- row_ids: int32 [8192, 8], P(('blk', 'table')), may hold values from 0 to 8191
Outputs:
- loss: float32 [8192], P(('blk', 'table'))
- item_grad: float32 [8192, 256], P(('blk', 'table'))
- query_grad: float32 [8192, 256], P(('blk', 'table'))
The draws below stay inside these ranges and needn't reach their ends.
Inputs may be any that keep to these rules, and one draw needn't show every extreme that they name: `owner_ids`: the 8 ids of one pair name 8 different shards; among the ids of one device's 256 pairs no shard is named more than 192 times, a bound that some block reaches.
All inputs are finite; a program needn't handle non-finite values.
Results may differ from the reference program's by a relative error of at most 0.0056.
Values may be sent and summed in bfloat16 or wider, within the bound.
No kernel may reach another device: no remote copies, remote signals or barrier semaphores. Data moves between devices by JAX's collectives and lax.ppermute only.
A program may use at most 64 MiB of HBM per device.

```python
import math
import jax
import jax.numpy as jnp
import numpy as np
from jax import lax

E = 256
H = 4096
B_DEV = 256
BAGS = 8
ROWS_DEV = 8192
CAP = 192
PAIRS = 8192
ROWS = 131072
N_BLK = 2
N_TABLE = 16


def set_ends(drawn, own_key, low, top_value):
    dims = drawn.shape
    spot = [jax.random.randint(jax.random.fold_in(own_key, axis), (), 0, dims[axis]) for axis in range(len(dims))]
    drawn = drawn.at[tuple(spot)].set(low)
    longest = dims.index(max(dims))
    spot[longest] = (spot[longest] + 1) % dims[longest]
    return drawn.at[tuple(spot)].set(top_value)


def levels(stream_key, shape, cuts, low, high):
    gain, own = 1.0, jax.random.fold_in(stream_key, 6)
    for axis_at, blocks in cuts:
        draws = jnp.exp(jax.random.uniform(jax.random.fold_in(own, axis_at), (blocks,), jnp.float32, low / len(cuts), high / len(cuts)))
        gain = gain * jnp.repeat(draws, shape[axis_at] // blocks).reshape([-1 if axis == axis_at else 1 for axis in range(len(shape))])
    return gain


def routed_block(own_key, own, number, rows, amount, top, most, lean):
    order = jax.random.permutation(own_key, amount)
    packed, usual = portions_of(amount, rows * top, most, lean, True), portions_of(amount, rows * top, most, lean, False)
    places = jnp.arange(amount)

    def named(lengths, offset_by):
        used = int((lengths > 0).sum())
        fixed = max(1, used // 4)
        moved = fixed + (places - fixed + offset_by * (used - fixed)) % max(1, amount - fixed)
        return jnp.zeros((amount,), jnp.int32).at[order[jnp.where(places < fixed, places, moved)]].set(jnp.asarray(lengths, jnp.int32))

    lengths = jnp.where(number % 4 == 0, named(packed, number // 4), named(usual, number - number // 4 - 1))
    mixed = jax.random.permutation(jax.random.fold_in(own, 3), amount)
    source_of, sink = mixed[0:amount // 2 * 2:2], mixed[1:amount // 2 * 2:2]
    margin = jnp.minimum(lengths[source_of] - 1, most - lengths[sink]) // 2
    margin = jnp.where((source_of == order[0]) | (sink == order[0]) | (lengths[sink] == 0), 0, jnp.maximum(margin, 0))
    moved = jax.random.randint(jax.random.fold_in(own, 4), (amount // 2,), 0, 1 << 20) % (margin + 1)
    lengths = lengths.at[source_of].add(-moved).at[sink].add(moved)
    members = jnp.searchsorted(jnp.cumsum(lengths), jnp.arange(rows * top), side="right").astype(jnp.int32)
    table = members.reshape(top, rows).T
    table = table[jax.random.permutation(jax.random.fold_in(own, 1), rows)]
    offset_by = jax.random.randint(jax.random.fold_in(own, 2), (rows, 1), 0, top)
    return jnp.take_along_axis(table, (jnp.arange(top)[None, :] + offset_by) % top, axis=1)


def portions_of(number_of, total, bound, skew, full):
    loads = [(1 << 20) // math.isqrt(grade ** skew) + 1 for grade in range(1, number_of + 1)]
    largest = bound if full else min(bound, max(-(-total // number_of), total * loads[0] // sum(loads)))
    least = 1 if total - largest >= number_of - 1 else 0
    given, rest = [largest] + [least] * (number_of - 1), total - largest - least * (number_of - 1)
    while rest > 0:
        candidates = [i for i in range(1, number_of) if given[i] < largest] or [i for i in range(1, number_of) if given[i] < bound]
        whole, left = sum([loads[i] for i in candidates]), rest
        for i in candidates:
            addition = min(bound - given[i], max(1, left * loads[i] // whole), rest)
            given[i] = given[i] + addition
            rest = rest - addition
    return np.array(given)


def centred(stream_key, extent, width, reach, cuts=(), dtype=jnp.bfloat16):
    values = jax.random.normal(stream_key, extent, jnp.float32) * width
    if len(cuts) > 0:
        values = levels(stream_key, extent, cuts, -0.22, 0.18) * values
    return jnp.clip(values, min=-reach, max=reach).astype(dtype)


def setup_inputs(seed: int = 0) -> dict:
    key_of = jax.random.split(jax.random.key(seed), 6)
    id_table = centred(key_of[0], (ROWS, E), 1.0, 6.0, ((0, 16),))
    w_first = centred(key_of[1], (E, H), E ** -0.5, 0.375)
    w_second = centred(key_of[2], (H, E), H ** -0.5, 0.09375)
    owner_ids_keys = jax.random.split(jax.random.fold_in(key_of[3], 1), PAIRS // B_DEV)
    owner_ids_turns = jax.random.permutation(jax.random.fold_in(key_of[3], 3), PAIRS // B_DEV)
    owner_ids = jax.vmap(lambda own, number: routed_block(jax.random.fold_in(key_of[3], 2), own, number, B_DEV, N_TABLE, BAGS, CAP, 2))(owner_ids_keys, owner_ids_turns).reshape((PAIRS, BAGS))
    row_ids = set_ends(jax.random.randint(key_of[4], (PAIRS, BAGS), 0, ROWS_DEV), jax.random.fold_in(key_of[4], 1), 0, ROWS_DEV - 1).astype(jnp.int32)
    return {"id_table": id_table, "w_first": w_first, "w_second": w_second, "owner_ids": owner_ids, "row_ids": row_ids}


EPS = 1e-06
INV_TEMP = 20.0

def silu_slope(pre):
    sigma = jax.nn.sigmoid(pre)
    return sigma * (1.0 + pre * (1.0 - sigma))

def unit_rows(vectors):
    scale = lax.rsqrt(lax.optimization_barrier(jnp.sum(vectors * vectors, axis=-1, keepdims=True)) + EPS)
    return (vectors * scale, scale)

def unit_backward(grad, unit, scale):
    return scale * (grad - unit * lax.optimization_barrier(jnp.sum(unit * grad, axis=-1, keepdims=True)))

def row_dot(left, right):
    return lax.dot_general(left, right, (((1,), (1,)), ((), ())), preferred_element_type=jnp.float32)

def col_dot(left, right):
    return lax.dot_general(left, right, (((0,), (0,)), ((), ())), preferred_element_type=jnp.float32)

def reference(id_table, w_first, w_second, owner_ids, row_ids):
    half = BAGS // 2

    def regroup(values):
        shaped = values.reshape((N_BLK, N_TABLE, B_DEV) + values.shape[1:])
        shaped = jnp.swapaxes(shaped, 0, 1)
        return shaped.reshape((N_TABLE, N_BLK * B_DEV) + values.shape[1:])

    def ungroup(values):
        shaped = values.reshape((N_TABLE, N_BLK, B_DEV) + values.shape[2:])
        shaped = jnp.swapaxes(shaped, 0, 1)
        return shaped.reshape((PAIRS,) + values.shape[2:])

    def group(pieces):
        owners, rows = pieces
        flat = (owners * ROWS_DEV + rows).astype(jnp.int32)
        embedded = jnp.take(id_table, flat, axis=0).astype(jnp.float32)
        query_in = lax.optimization_barrier(jnp.sum(embedded[:, :half], axis=1)).astype(jnp.bfloat16)
        item_in = lax.optimization_barrier(jnp.sum(embedded[:, half:], axis=1))
        hidden_pre = jnp.dot(query_in, w_first, preferred_element_type=jnp.float32)
        hidden = jax.nn.silu(hidden_pre).astype(jnp.bfloat16)
        query_out = jnp.dot(hidden, w_second, preferred_element_type=jnp.float32)
        query_unit, query_scale = unit_rows(query_out)
        item_unit, item_scale = unit_rows(item_in)
        query_bf = query_unit.astype(jnp.bfloat16)
        item_bf = item_unit.astype(jnp.bfloat16)
        scores = INV_TEMP * row_dot(query_bf, item_bf)
        log_total = jnp.log(lax.optimization_barrier(jnp.sum(jnp.exp(scores), axis=1)))
        own = INV_TEMP * lax.optimization_barrier(jnp.sum(query_bf.astype(jnp.float32) * item_bf.astype(jnp.float32), axis=1))
        loss = log_total - own
        probs = jnp.exp(scores - log_total[:, None]).astype(jnp.bfloat16)
        query_sum = jnp.dot(probs, item_bf, preferred_element_type=jnp.float32)
        item_sum = col_dot(probs, query_bf)
        query_unit_grad = INV_TEMP * (query_sum - item_bf.astype(jnp.float32))
        item_unit_grad = INV_TEMP * (item_sum - query_bf.astype(jnp.float32))
        item_grad = unit_backward(item_unit_grad, item_unit, item_scale)
        out_grad = unit_backward(query_unit_grad, query_unit, query_scale).astype(jnp.bfloat16)
        hidden_grad = (row_dot(out_grad, w_second) * silu_slope(hidden_pre)).astype(jnp.bfloat16)
        query_grad = row_dot(hidden_grad, w_first)
        return (loss, item_grad, query_grad)
    loss, item_grad, query_grad = lax.map(group, (regroup(owner_ids), regroup(row_ids)))
    return (ungroup(loss), ungroup(item_grad), ungroup(query_grad))
```

```python
import functools

import jax
import jax.numpy as jnp
from jax import lax
from jax.experimental import pallas as pl
from jax.experimental.pallas import tpu as pltpu
from jax.sharding import PartitionSpec as P

EPS = 1e-06
INV_TEMP = 20.0


def params(mebibytes):
    return pltpu.CompilerParams(vmem_limit_bytes=mebibytes * 1024 * 1024)


def iota(shape, dim):
    return lax.broadcasted_iota(jnp.int32, shape, dim)


def row_dot(left, right):
    return lax.dot_general(
        left, right, (((1,), (1,)), ((), ())), preferred_element_type=jnp.float32
    )


def col_dot(left, right):
    return lax.dot_general(
        left, right, (((0,), (0,)), ((), ())), preferred_element_type=jnp.float32
    )


def dot(left, right):
    return jnp.dot(left, right, preferred_element_type=jnp.float32)


def unit_rows(vectors):
    scale = lax.rsqrt(jnp.sum(vectors * vectors, axis=-1, keepdims=True) + EPS)
    return vectors * scale, scale


def unit_backward(grad, unit, scale):
    return scale * (grad - unit * jnp.sum(unit * grad, axis=-1, keepdims=True))


def route_kernel(relative, rows_dev, *refs):
    codes, near_ref, far_ref, request_refs = refs[:4], refs[4], refs[5], refs[6:]
    chips = len(request_refs)
    bags, pairs = codes[0].shape
    capacity = near_ref.shape[1]
    lists = 6 * chips
    place = lax.axis_index("table")
    half = 2 * chips
    list_of = iota((lists, pairs), 0)
    chip = relative(place % half // 2, list_of % chips)
    asker = list_of // chips
    core = jnp.where(asker < 4, place % 2, 1 - place % 2)
    start = (place // half * half + chip * 2 + core) * rows_dev
    named = jnp.zeros((lists, pairs), jnp.float32)
    rows = jnp.zeros((lists, pairs), jnp.int32)
    kind = jnp.zeros((lists, pairs), jnp.int32)
    for k in range(bags):
        code = codes[0][k : k + 1, :]
        for r, at in ((1, 1), (2, 2), (3, 3), (5, 2)):
            code = jnp.where(asker == r, codes[at][k : k + 1, :], code)
        row = code - start
        hit = (row >= 0) & (row < rows_dev)
        named = jnp.where(hit, 1.0, named)
        rows = jnp.where(hit, row, rows)
        kind = jnp.where(hit, 1 if k < bags // 2 else 2, kind)
    before = jnp.where(iota((pairs, pairs), 0) < iota((pairs, pairs), 1), 1.0, 0.0)
    slot = dot(named.astype(jnp.bfloat16), before.astype(jnp.bfloat16)).astype(jnp.int32)
    slot = jnp.where(named > 0.0, slot, -1)
    digits = [rows // 256, rows % 256, kind, iota((lists, pairs), 1)]
    packed = jnp.concatenate([d.astype(jnp.float32) for d in digits], axis=0).astype(jnp.bfloat16)
    places = iota((capacity, pairs), 0)
    for s in range(lists):
        chosen = jnp.where(slot[s : s + 1, :] == places, 1.0, 0.0).astype(jnp.bfloat16)
        got = row_dot(packed, chosen).astype(jnp.int32)
        high, low, which, pair = [got[i * lists + s : i * lists + s + 1, :] for i in range(4)]
        asked, j = s // chips, s % chips
        if asked < 4:
            request_refs[j][asked : asked + 1, :] = 2 * (high * 256 + low)
        if asked in (0, 2, 4, 5):
            at = j if asked < 4 else chips + j
            bag_ref = near_ref if asked in (0, 4) else far_ref
            bag_ref[at : at + 1, :] = (which - 1) * pairs + pair


def widen_kernel(table_ref, wide_ref):
    width = table_ref.shape[1]
    step = 128

    def widen(i, carry):
        start = pl.multiple_of(i * step, step)
        part = table_ref[pl.ds(start, step), :].astype(jnp.float32)
        wide_ref[pl.ds(2 * start, step, stride=2), :] = part[:, : width // 2]
        wide_ref[pl.ds(2 * start + 1, step, stride=2), :] = part[:, width // 2 :]
        return carry

    lax.fori_loop(0, table_ref.shape[0] // step, widen, 0)


def gather_kernel(chips, asker, *refs):
    wanted, wide_ref, out_ref, stage = refs[:chips], refs[chips], refs[chips + 1], refs[-1]
    _, capacity, width = out_ref.shape
    group = 16
    for j in range(chips):
        index_ref = wanted[chips - 1 - j]
        for base in range(0, capacity, group):
            found = [wide_ref[pl.ds(index_ref[asker, base + i], 2), :] for i in range(group)]
            for i in range(group):
                stage[pl.ds(2 * (base + i), 2), :] = found[i]
        for part in range(2):
            values = stage[pl.ds(part, capacity, stride=2), :]
            out_ref[j, :, part * (width // 2) : (part + 1) * (width // 2)] = values.astype(
                jnp.bfloat16
            )


def pack_kernel(chips, same_ref, swapped_ref, *out_refs):
    for out_ref, j in zip(out_refs, range(chips - 1, 0, -1)):
        out_ref[0] = same_ref[j]
        out_ref[1] = swapped_ref[j]


def bag_sums(bag_ref, rows, bags):
    total = None
    for at, values in enumerate(rows):
        chosen = bag_ref[at : at + 1, :] == iota((bags, bag_ref.shape[1]), 0)
        part = dot(jnp.where(chosen, 1.0, 0.0).astype(jnp.bfloat16), values)
        total = part if total is None else total + part
    return total


def lists_of(order, same_ref, swapped_ref, message_refs):
    chips = len(order) + 1
    return [
        own_ref[0] if j == 0 else message_refs[order.index(j)][f]
        for f, own_ref in enumerate((same_ref, swapped_ref))
        for j in range(chips)
    ]


def far_kernel(order, bag_ref, same_ref, swapped_ref, *refs):
    messages, (query_ref, item_ref) = refs[:-2], refs[-2:]
    pairs = query_ref.shape[0]
    total = bag_sums(bag_ref, lists_of(order, same_ref, swapped_ref, messages), 2 * pairs)
    query_ref[...] = total[:pairs].astype(jnp.bfloat16)
    item_ref[...] = total[pairs:].astype(jnp.bfloat16)


def item_kernel(order, bag_ref, far_ref, same_ref, swapped_ref, *refs):
    messages, (query_ref, unit_ref, scale_ref, bf_ref) = refs[:-4], refs[-4:]
    pairs = query_ref.shape[0]
    total = bag_sums(bag_ref, lists_of(order, same_ref, swapped_ref, messages), 2 * pairs)
    query_ref[...] = total[:pairs]
    unit, scale = unit_rows(total[pairs:] + far_ref[...].astype(jnp.float32))
    unit_ref[...] = unit
    scale_ref[...] = scale
    bf_ref[...] = unit.astype(jnp.bfloat16)


def tower_kernel(
    near_ref, far_ref, first_ref, second_ref, unit_ref, scale_ref, bf_ref, slope_ref
):
    query_in = (near_ref[...] + far_ref[...].astype(jnp.float32)).astype(jnp.bfloat16)
    step = 1024
    total = None
    for at in range(0, first_ref.shape[1], step):
        pre = dot(query_in, first_ref[:, at : at + step])
        sigma = 1.0 / (1.0 + jnp.exp(-pre))
        hidden = pre * sigma
        slope_ref[:, at : at + step] = sigma * (1.0 + pre * (1.0 - sigma))
        part = dot(hidden.astype(jnp.bfloat16), second_ref[at : at + step, :])
        total = part if total is None else total + part
    unit, scale = unit_rows(total)
    unit_ref[...] = unit
    scale_ref[...] = scale
    bf_ref[...] = unit.astype(jnp.bfloat16)


def group_exps(query, item):
    return jnp.exp(INV_TEMP * row_dot(query, item))


def row_sums(values):
    return jnp.sum(values, axis=1, keepdims=True)


def query_grad_kernel(blocks, *refs):
    query_ref, items, refs = refs[0], refs[1 : 1 + blocks], refs[1 + blocks :]
    first_ref, second_ref, slope_ref, unit_ref, scale_ref, loss_ref, grad_ref, item_sum_ref = refs
    query = query_ref[...]
    kept = [group_exps(query, item[...]) for item in items[:2]]
    total = sum(row_sums(exps) for exps in kept)
    for item in items[2:]:
        total = total + row_sums(group_exps(query, item[...]))
    inverse = 1.0 / total
    query_sum = jnp.zeros(query.shape, jnp.float32)
    for j, item in enumerate(items):
        exps = kept[j] if j < 2 else group_exps(query, item[...])
        probs = (exps * inverse).astype(jnp.bfloat16)
        query_sum = query_sum + dot(probs, item[...])
        if j == 0:
            item_sum_ref[...] = col_dot(probs, query)
    wide_item = items[0][...].astype(jnp.float32)
    own = INV_TEMP * row_sums(query.astype(jnp.float32) * wide_item)
    loss_ref[...] = (jnp.log(total) - own).T
    out_grad = unit_backward(
        INV_TEMP * (query_sum - wide_item), unit_ref[...], scale_ref[...]
    ).astype(jnp.bfloat16)
    step = 1024
    total = None
    for at in range(0, first_ref.shape[1], step):
        back = row_dot(out_grad, second_ref[at : at + step, :])
        hidden_grad = (back * slope_ref[:, at : at + step]).astype(jnp.bfloat16)
        part = row_dot(hidden_grad, first_ref[:, at : at + step])
        total = part if total is None else total + part
    grad_ref[...] = total


def item_grad_kernel(blocks, *refs):
    queries, items, refs = refs[:blocks], refs[blocks : 2 * blocks], refs[2 * blocks :]
    item_sum_ref, unit_ref, scale_ref, grad_ref, all_queries, all_items = refs
    for b in range(blocks):
        all_queries[b] = queries[b][...]
        all_items[b] = items[b][...]
    own_item = all_items[0]

    def add(i, total):
        query = all_queries[i]
        own_exps = group_exps(query, own_item)

        def add_total(j, sums):
            return sums + row_sums(group_exps(query, all_items[j]))

        sums = lax.fori_loop(1, blocks, add_total, row_sums(own_exps), unroll=blocks == 2)
        probs = (own_exps * (1.0 / sums)).astype(jnp.bfloat16)
        return total + col_dot(probs, query)

    item_sum = lax.fori_loop(1, blocks, add, item_sum_ref[...], unroll=blocks == 2)
    grad_ref[...] = unit_backward(
        INV_TEMP * (item_sum - all_queries[0].astype(jnp.float32)), unit_ref[...], scale_ref[...]
    )


def rotated(shard, axis, by):
    count = lax.axis_size(axis)
    return lax.ppermute(shard, axis, [(i, (i + by) % count) for i in range(count)])


def struct(shape, dtype):
    return jax.ShapeDtypeStruct(shape, dtype)


def local(id_table, w_first, w_second, owner_ids, row_ids):
    pairs, bags = owner_ids.shape
    shards = lax.axis_size("table")
    blocks = lax.axis_size("blk")
    width = id_table.shape[1]
    hidden_units = w_first.shape[1]
    capacity = min(pairs, 3 * pairs * bags // (2 * shards))
    bf, f32 = jnp.bfloat16, jnp.float32

    half = shards // 2
    chips = half // 2
    power = chips & (chips - 1) == 0

    def relative(chip, j):
        return chip ^ j if power else (chip + j) % chips

    def to_chip(values, j, flip=0):
        if j == 0 and flip == 0:
            return values
        route = [
            (t, t // half * half + relative(t % half // 2, j) * 2 + (t % 2 ^ flip))
            for t in range(shards)
        ]
        return lax.ppermute(values, "table", route)

    def to_mirror(values, flip=0):
        route = [(t, ((t + half) % shards) ^ flip) for t in range(shards)]
        return lax.ppermute(values, "table", route)

    code = owner_ids * id_table.shape[0] + row_ids
    codes = [code, to_chip(code, 0, 1), to_mirror(code), to_mirror(code, 1)]
    wide = pl.pallas_call(
        widen_kernel,
        out_shape=struct((2 * id_table.shape[0], width // 2), f32),
        compiler_params=params(8),
        name="widen",
    )(id_table)
    *codes, wide = lax.optimization_barrier((*codes, wide))
    near_bags, far_bags, *requests = pl.pallas_call(
        functools.partial(route_kernel, relative, id_table.shape[0]),
        out_shape=[struct((half, capacity), jnp.int32)] * 2
        + [struct((4, capacity), jnp.int32)] * chips,
        compiler_params=params(4),
        name="route",
    )(*[c.T for c in codes])
    wanted = [to_chip(requests[j], j) for j in reversed(range(chips))][::-1]

    def gather(asker, wide):
        return pl.pallas_call(
            functools.partial(gather_kernel, chips, asker),
            in_specs=[pl.BlockSpec(memory_space=pltpu.SMEM)] * chips
            + [pl.BlockSpec(memory_space=pltpu.VMEM)],
            out_shape=struct((chips, capacity, width), bf),
            scratch_shapes=[pltpu.VMEM((2 * capacity, width // 2), f32)],
            compiler_params=params(8),
            name="gather",
        )(*wanted[::-1], wide)

    def answered(first, wide, order):
        swapped = to_chip(gather(first + 1, wide), 0, 1)
        same = gather(first, wide)
        messages = pl.pallas_call(
            functools.partial(pack_kernel, chips),
            out_shape=[struct((2, capacity, width), bf)] * (chips - 1),
            compiler_params=params(8),
            name="pack",
        )(same, swapped)
        arrived = []
        for j in order:
            back = j if power else (chips - j) % chips
            arrived.append(to_chip(messages[chips - 1 - back], back))
        return (same, swapped, *arrived), messages

    order = list(range(chips - 1, 0, -1))
    far_rows, far_messages = answered(2, wide, order)
    wide, _ = lax.optimization_barrier((wide, far_messages[-1]))
    near_rows, near_messages = answered(0, wide, order)
    far_bags, _ = lax.optimization_barrier((far_bags, near_messages[-1]))
    far_query, far_item = pl.pallas_call(
        functools.partial(far_kernel, order),
        out_shape=[struct((pairs, width), bf)] * 2,
        compiler_params=params(8),
        name="far_bags",
    )(far_bags, *far_rows)
    far_item = to_mirror(far_item)
    far_query = to_mirror(far_query)
    near_query, item_unit, item_scale, item_bf = pl.pallas_call(
        functools.partial(item_kernel, order),
        out_shape=[
            struct((pairs, width), f32),
            struct((pairs, width), f32),
            struct((pairs, 1), f32),
            struct((pairs, width), bf),
        ],
        compiler_params=params(8),
        name="items",
    )(near_bags, far_item, *near_rows)
    items = [item_bf] + [rotated(item_bf, "blk", by) for by in range(1, blocks)]
    query_unit, query_scale, query_bf, slope = pl.pallas_call(
        tower_kernel,
        out_shape=[
            struct((pairs, width), f32),
            struct((pairs, 1), f32),
            struct((pairs, width), bf),
            struct((pairs, hidden_units), f32),
        ],
        compiler_params=params(12),
        name="tower",
    )(near_query, far_query, w_first, w_second)
    queries = [query_bf] + [rotated(query_bf, "blk", by) for by in range(1, blocks)]
    loss, query_grad, own_sum = pl.pallas_call(
        functools.partial(query_grad_kernel, blocks),
        out_shape=[
            struct((1, pairs), f32),
            struct((pairs, width), f32),
            struct((pairs, width), f32),
        ],
        compiler_params=params(12),
        name="query_grads",
    )(query_bf, *items, w_first, w_second, slope, query_unit, query_scale)
    item_grad = pl.pallas_call(
        functools.partial(item_grad_kernel, blocks),
        out_shape=struct((pairs, width), f32),
        scratch_shapes=[pltpu.VMEM((blocks, pairs, width), bf)] * 2,
        compiler_params=params(12),
        name="item_grads",
    )(*queries, *items, own_sum, item_unit, item_scale)
    return loss.reshape(pairs), item_grad, query_grad


def solution(mesh):
    placed = (P("table", None), P(), P(), P(("blk", "table"), None), P(("blk", "table"), None))
    return jax.shard_map(
        local,
        mesh=mesh,
        in_specs=placed,
        out_specs=(P(("blk", "table")), P(("blk", "table"), None), P(("blk", "table"), None)),
        check_vma=False,
    )
```

```python
import functools

import jax
import jax.numpy as jnp
from jax import lax
from jax.experimental import pallas as pl
from jax.experimental.pallas import tpu as pltpu
from jax.sharding import PartitionSpec as P

EPS = 1e-06
INV_TEMP = 20.0


def params(mebibytes):
    return pltpu.CompilerParams(vmem_limit_bytes=mebibytes * 1024 * 1024)


def iota(shape, dim):
    return lax.broadcasted_iota(jnp.int32, shape, dim)


def row_dot(left, right):
    return lax.dot_general(
        left, right, (((1,), (1,)), ((), ())), preferred_element_type=jnp.float32
    )


def col_dot(left, right):
    return lax.dot_general(
        left, right, (((0,), (0,)), ((), ())), preferred_element_type=jnp.float32
    )


def dot(left, right):
    return jnp.dot(left, right, preferred_element_type=jnp.float32)


def unit_rows(vectors):
    scale = lax.rsqrt(jnp.sum(vectors * vectors, axis=-1, keepdims=True) + EPS)
    return vectors * scale, scale


def unit_backward(grad, unit, scale):
    return scale * (grad - unit * jnp.sum(unit * grad, axis=-1, keepdims=True))


def route_kernel(relative, rows_dev, *refs):
    codes, near_ref, far_ref, request_refs = refs[:4], refs[4], refs[5], refs[6:]
    chips = len(request_refs)
    bags, pairs = codes[0].shape
    capacity = near_ref.shape[1]
    lists = 6 * chips
    place = lax.axis_index("table")
    half = 2 * chips
    list_of = iota((lists, pairs), 0)
    chip = relative(place % half // 2, list_of % chips)
    asker = list_of // chips
    core = jnp.where(asker < 4, place % 2, 1 - place % 2)
    start = (place // half * half + chip * 2 + core) * rows_dev
    named = jnp.zeros((lists, pairs), jnp.float32)
    rows = jnp.zeros((lists, pairs), jnp.int32)
    kind = jnp.zeros((lists, pairs), jnp.int32)
    for k in range(bags):
        code = codes[0][k : k + 1, :]
        for r, at in ((1, 1), (2, 2), (3, 3), (5, 2)):
            code = jnp.where(asker == r, codes[at][k : k + 1, :], code)
        row = code - start
        hit = (row >= 0) & (row < rows_dev)
        named = jnp.where(hit, 1.0, named)
        rows = jnp.where(hit, row, rows)
        kind = jnp.where(hit, 1 if k < bags // 2 else 2, kind)
    before = jnp.where(iota((pairs, pairs), 0) < iota((pairs, pairs), 1), 1.0, 0.0)
    slot = dot(named.astype(jnp.bfloat16), before.astype(jnp.bfloat16)).astype(jnp.int32)
    slot = jnp.where(named > 0.0, slot, -1)
    digits = [rows // 256, rows % 256, kind, iota((lists, pairs), 1)]
    packed = jnp.concatenate([d.astype(jnp.float32) for d in digits], axis=0).astype(jnp.bfloat16)
    places = iota((capacity, pairs), 0)
    for s in range(lists):
        chosen = jnp.where(slot[s : s + 1, :] == places, 1.0, 0.0).astype(jnp.bfloat16)
        got = row_dot(packed, chosen).astype(jnp.int32)
        high, low, which, pair = [got[i * lists + s : i * lists + s + 1, :] for i in range(4)]
        asked, j = s // chips, s % chips
        if asked < 4:
            request_refs[j][asked : asked + 1, :] = 2 * (high * 256 + low)
        if asked in (0, 2, 4, 5):
            at = j if asked < 4 else chips + j
            bag_ref = near_ref if asked in (0, 4) else far_ref
            bag_ref[at : at + 1, :] = (which - 1) * pairs + pair


def widen_kernel(table_ref, wide_ref):
    width = table_ref.shape[1]
    step = 128

    def widen(i, carry):
        start = pl.multiple_of(i * step, step)
        part = table_ref[pl.ds(start, step), :].astype(jnp.float32)
        wide_ref[pl.ds(2 * start, step, stride=2), :] = part[:, : width // 2]
        wide_ref[pl.ds(2 * start + 1, step, stride=2), :] = part[:, width // 2 :]
        return carry

    lax.fori_loop(0, table_ref.shape[0] // step, widen, 0)


def gather_kernel(chips, askers, *refs):
    wanted, wide_ref, refs = refs[:chips], refs[chips], refs[chips + 1 :]
    outs, (index_ref, stage, sems) = refs[: len(askers)], refs[len(askers) :]
    _, capacity, width = outs[0].shape
    group = 16
    copies = [
        pltpu.make_async_copy(wanted[chips - 1 - j], index_ref.at[j], sems.at[j])
        for j in range(chips)
    ]
    for copy in copies:
        copy.start()
    for copy in copies:
        copy.wait()
    for asker, out_ref in zip(askers, outs):
        for j in range(chips):
            for base in range(0, capacity, group):
                found = [
                    wide_ref[pl.ds(index_ref[j, asker, base + i], 2), :] for i in range(group)
                ]
                for i in range(group):
                    stage[pl.ds(2 * (base + i), 2), :] = found[i]
            for part in range(2):
                values = stage[pl.ds(part, capacity, stride=2), :]
                out_ref[j, :, part * (width // 2) : (part + 1) * (width // 2)] = values.astype(
                    jnp.bfloat16
                )


def pack_kernel(chips, same_ref, swapped_ref, *out_refs):
    for out_ref, j in zip(out_refs, range(chips - 1, 0, -1)):
        out_ref[0] = same_ref[j]
        out_ref[1] = swapped_ref[j]


def bag_sums(bag_ref, rows, bags):
    total = None
    for at, values in enumerate(rows):
        chosen = bag_ref[at : at + 1, :] == iota((bags, bag_ref.shape[1]), 0)
        part = dot(jnp.where(chosen, 1.0, 0.0).astype(jnp.bfloat16), values)
        total = part if total is None else total + part
    return total


def lists_of(order, same_ref, swapped_ref, message_refs):
    chips = len(order) + 1
    return [
        own_ref[0] if j == 0 else message_refs[order.index(j)][f]
        for f, own_ref in enumerate((same_ref, swapped_ref))
        for j in range(chips)
    ]


def far_kernel(order, bag_ref, same_ref, swapped_ref, *refs):
    messages, (query_ref, item_ref) = refs[:-2], refs[-2:]
    pairs = query_ref.shape[0]
    total = bag_sums(bag_ref, lists_of(order, same_ref, swapped_ref, messages), 2 * pairs)
    query_ref[...] = total[:pairs].astype(jnp.bfloat16)
    item_ref[...] = total[pairs:].astype(jnp.bfloat16)


def item_kernel(order, bag_ref, far_ref, same_ref, swapped_ref, *refs):
    messages, (query_ref, unit_ref, scale_ref, bf_ref) = refs[:-4], refs[-4:]
    pairs = query_ref.shape[0]
    total = bag_sums(bag_ref, lists_of(order, same_ref, swapped_ref, messages), 2 * pairs)
    query_ref[...] = total[:pairs]
    unit, scale = unit_rows(total[pairs:] + far_ref[...].astype(jnp.float32))
    unit_ref[...] = unit
    scale_ref[...] = scale
    bf_ref[...] = unit.astype(jnp.bfloat16)


def tower_kernel(
    near_ref, far_ref, first_ref, second_ref, unit_ref, scale_ref, bf_ref, slope_ref
):
    query_in = (near_ref[...] + far_ref[...].astype(jnp.float32)).astype(jnp.bfloat16)
    step = 1024
    total = None
    for at in range(0, first_ref.shape[1], step):
        pre = dot(query_in, first_ref[:, at : at + step])
        sigma = 0.5 + 0.5 * jnp.tanh(0.5 * pre)
        hidden = pre * sigma
        slope_ref[:, at : at + step] = sigma * (1.0 + pre * (1.0 - sigma))
        part = dot(hidden.astype(jnp.bfloat16), second_ref[at : at + step, :])
        total = part if total is None else total + part
    unit, scale = unit_rows(total)
    unit_ref[...] = unit
    scale_ref[...] = scale
    bf_ref[...] = unit.astype(jnp.bfloat16)


def group_exps(query, item):
    return jnp.exp(INV_TEMP * row_dot(query, item))


def row_sums(values):
    return jnp.sum(values, axis=1, keepdims=True)


def query_grad_kernel(blocks, *refs):
    query_ref, items, refs = refs[0], refs[1 : 1 + blocks], refs[1 + blocks :]
    first_ref, second_ref, slope_ref, unit_ref, scale_ref, loss_ref, grad_ref, item_sum_ref = refs
    query = query_ref[...]
    kept = [group_exps(query, item[...]) for item in items[:2]]
    total = sum(row_sums(exps) for exps in kept)
    for item in items[2:]:
        total = total + row_sums(group_exps(query, item[...]))
    inverse = 1.0 / total
    query_sum = jnp.zeros(query.shape, jnp.float32)
    for j, item in enumerate(items):
        exps = kept[j] if j < 2 else group_exps(query, item[...])
        probs = (exps * inverse).astype(jnp.bfloat16)
        query_sum = query_sum + dot(probs, item[...])
        if j == 0:
            item_sum_ref[...] = col_dot(probs, query)
    wide_item = items[0][...].astype(jnp.float32)
    own = INV_TEMP * row_sums(query.astype(jnp.float32) * wide_item)
    loss_ref[...] = (jnp.log(total) - own).T
    out_grad = unit_backward(
        INV_TEMP * (query_sum - wide_item), unit_ref[...], scale_ref[...]
    ).astype(jnp.bfloat16)
    step = 1024
    total = None
    for at in range(0, first_ref.shape[1], step):
        back = row_dot(out_grad, second_ref[at : at + step, :])
        hidden_grad = (back * slope_ref[:, at : at + step]).astype(jnp.bfloat16)
        part = row_dot(hidden_grad, first_ref[:, at : at + step])
        total = part if total is None else total + part
    grad_ref[...] = total


def item_grad_kernel(blocks, *refs):
    queries, items, refs = refs[:blocks], refs[blocks : 2 * blocks], refs[2 * blocks :]
    item_sum_ref, unit_ref, scale_ref, grad_ref = refs
    item_sum = item_sum_ref[...]
    for i in range(1, blocks):
        query = queries[i][...]
        own_exps = group_exps(query, items[0][...])
        total = row_sums(own_exps)
        for j in range(1, blocks):
            total = total + row_sums(group_exps(query, items[j][...]))
        item_sum = item_sum + col_dot((own_exps * (1.0 / total)).astype(jnp.bfloat16), query)
    grad_ref[...] = unit_backward(
        INV_TEMP * (item_sum - queries[0][...].astype(jnp.float32)), unit_ref[...], scale_ref[...]
    )


def rotated(shard, axis, by):
    count = lax.axis_size(axis)
    return lax.ppermute(shard, axis, [(i, (i + by) % count) for i in range(count)])


def struct(shape, dtype):
    return jax.ShapeDtypeStruct(shape, dtype)


def local(id_table, w_first, w_second, owner_ids, row_ids):
    pairs, bags = owner_ids.shape
    shards = lax.axis_size("table")
    blocks = lax.axis_size("blk")
    width = id_table.shape[1]
    hidden_units = w_first.shape[1]
    capacity = min(pairs, 3 * pairs * bags // (2 * shards))
    bf, f32 = jnp.bfloat16, jnp.float32

    half = shards // 2
    chips = half // 2
    power = chips & (chips - 1) == 0

    def relative(chip, j):
        return chip ^ j if power else (chip + j) % chips

    def to_chip(values, j, flip=0):
        if j == 0 and flip == 0:
            return values
        route = [
            (t, t // half * half + relative(t % half // 2, j) * 2 + (t % 2 ^ flip))
            for t in range(shards)
        ]
        return lax.ppermute(values, "table", route)

    def to_mirror(values):
        return lax.ppermute(values, "table", [(t, (t + half) % shards) for t in range(shards)])

    code = owner_ids * id_table.shape[0] + row_ids
    mirror_code = to_mirror(code)
    codes = [code, to_chip(code, 0, 1), mirror_code, to_chip(mirror_code, 0, 1)]
    wide = pl.pallas_call(
        widen_kernel,
        out_shape=struct((2 * id_table.shape[0], width // 2), f32),
        compiler_params=params(8),
        name="widen",
    )(id_table)
    near_bags, far_bags, *requests = pl.pallas_call(
        functools.partial(route_kernel, relative, id_table.shape[0]),
        out_shape=[struct((half, capacity), jnp.int32)] * 2
        + [struct((4, capacity), jnp.int32)] * chips,
        compiler_params=params(4),
        name="route",
    )(*[c.T for c in codes])
    wanted = [to_chip(requests[j], j) for j in reversed(range(chips))][::-1]

    def gather(askers):
        return pl.pallas_call(
            functools.partial(gather_kernel, chips, askers),
            in_specs=[pl.BlockSpec(memory_space=pl.ANY)] * chips
            + [pl.BlockSpec(memory_space=pltpu.VMEM)],
            out_shape=[struct((chips, capacity, width), bf)] * len(askers),
            scratch_shapes=[
                pltpu.SMEM((chips, 4, capacity), jnp.int32),
                pltpu.VMEM((2 * capacity, width // 2), f32),
                pltpu.SemaphoreType.DMA((chips,)),
            ],
            compiler_params=params(8),
            name="gather",
        )(*wanted[::-1], wide)

    order = list(range(chips - 1, 0, -1))

    def answered(same, swapped):
        messages = pl.pallas_call(
            functools.partial(pack_kernel, chips),
            out_shape=[struct((2, capacity, width), bf)] * (chips - 1),
            compiler_params=params(8),
            name="pack",
        )(same, swapped)
        arrived = []
        for j in order:
            back = j if power else (chips - j) % chips
            arrived.append(to_chip(messages[chips - 1 - back], back))
        return (same, swapped, *arrived), messages

    far_other, near_other = [to_chip(rows, 0, 1) for rows in gather((3, 1))]
    far_same, near_same = gather((2, 0))
    far_rows, _ = answered(far_same, far_other)
    near_rows, near_messages = answered(near_same, near_other)
    far_bags, _ = lax.optimization_barrier((far_bags, near_messages[-1]))
    far_query, far_item = pl.pallas_call(
        functools.partial(far_kernel, order),
        out_shape=[struct((pairs, width), bf)] * 2,
        compiler_params=params(8),
        name="far_bags",
    )(far_bags, *far_rows)
    far_item = to_mirror(far_item)
    far_query = to_mirror(far_query)
    near_query, item_unit, item_scale, item_bf = pl.pallas_call(
        functools.partial(item_kernel, order),
        out_shape=[
            struct((pairs, width), f32),
            struct((pairs, width), f32),
            struct((pairs, 1), f32),
            struct((pairs, width), bf),
        ],
        compiler_params=params(8),
        name="items",
    )(near_bags, far_item, *near_rows)
    items = [item_bf] + [rotated(item_bf, "blk", by) for by in range(1, blocks)]
    query_unit, query_scale, query_bf, slope = pl.pallas_call(
        tower_kernel,
        out_shape=[
            struct((pairs, width), f32),
            struct((pairs, 1), f32),
            struct((pairs, width), bf),
            struct((pairs, hidden_units), f32),
        ],
        compiler_params=params(12),
        name="tower",
    )(near_query, far_query, w_first, w_second)
    queries = [query_bf] + [rotated(query_bf, "blk", by) for by in range(1, blocks)]
    loss, query_grad, own_sum = pl.pallas_call(
        functools.partial(query_grad_kernel, blocks),
        out_shape=[
            struct((1, pairs), f32),
            struct((pairs, width), f32),
            struct((pairs, width), f32),
        ],
        compiler_params=params(12),
        name="query_grads",
    )(query_bf, *items, w_first, w_second, slope, query_unit, query_scale)
    item_grad = pl.pallas_call(
        functools.partial(item_grad_kernel, blocks),
        out_shape=struct((pairs, width), f32),
        compiler_params=params(12),
        name="item_grads",
    )(*queries, *items, own_sum, item_unit, item_scale)
    return loss.reshape(pairs), item_grad, query_grad


def solution(mesh):
    placed = (P("table", None), P(), P(), P(("blk", "table"), None), P(("blk", "table"), None))
    return jax.shard_map(
        local,
        mesh=mesh,
        in_specs=placed,
        out_specs=(P(("blk", "table")), P(("blk", "table"), None), P(("blk", "table"), None)),
        check_vma=False,
    )
```

```python
import functools

import jax
import jax.numpy as jnp
from jax import lax
from jax.experimental import pallas as pl
from jax.experimental.pallas import tpu as pltpu
from jax.sharding import PartitionSpec as P

EPS = 1e-06
INV_TEMP = 20.0


def params(mebibytes):
    return pltpu.CompilerParams(vmem_limit_bytes=mebibytes * 1024 * 1024)


def iota(shape, dim):
    return lax.broadcasted_iota(jnp.int32, shape, dim)


def row_dot(left, right):
    return lax.dot_general(
        left, right, (((1,), (1,)), ((), ())), preferred_element_type=jnp.float32
    )


def col_dot(left, right):
    return lax.dot_general(
        left, right, (((0,), (0,)), ((), ())), preferred_element_type=jnp.float32
    )


def dot(left, right):
    return jnp.dot(left, right, preferred_element_type=jnp.float32)


def unit_rows(vectors):
    scale = lax.rsqrt(jnp.sum(vectors * vectors, axis=-1, keepdims=True) + EPS)
    return vectors * scale, scale


def unit_backward(grad, unit, scale):
    return scale * (grad - unit * jnp.sum(unit * grad, axis=-1, keepdims=True))


def route_kernel(relative, rows_dev, *refs):
    codes, near_ref, far_ref, request_refs = refs[:4], refs[4], refs[5], refs[6:]
    chips = len(request_refs)
    bags, pairs = codes[0].shape
    capacity = near_ref.shape[1]
    lists = 6 * chips
    place = lax.axis_index("table")
    half = 2 * chips
    list_of = iota((lists, pairs), 0)
    chip = relative(place % half // 2, list_of % chips)
    asker = list_of // chips
    core = jnp.where(asker < 4, place % 2, 1 - place % 2)
    start = (place // half * half + chip * 2 + core) * rows_dev
    named = jnp.zeros((lists, pairs), jnp.float32)
    rows = jnp.zeros((lists, pairs), jnp.int32)
    kind = jnp.zeros((lists, pairs), jnp.int32)
    for k in range(bags):
        code = codes[0][k : k + 1, :]
        for r, at in ((1, 1), (2, 2), (3, 3), (5, 2)):
            code = jnp.where(asker == r, codes[at][k : k + 1, :], code)
        row = code - start
        hit = (row >= 0) & (row < rows_dev)
        named = jnp.where(hit, 1.0, named)
        rows = jnp.where(hit, row, rows)
        kind = jnp.where(hit, 1 if k < bags // 2 else 2, kind)
    before = jnp.where(iota((pairs, pairs), 0) < iota((pairs, pairs), 1), 1.0, 0.0)
    slot = dot(named.astype(jnp.bfloat16), before.astype(jnp.bfloat16)).astype(jnp.int32)
    slot = jnp.where(named > 0.0, slot, -1)
    digits = [rows // 256, rows % 256, kind, iota((lists, pairs), 1)]
    packed = jnp.concatenate([d.astype(jnp.float32) for d in digits], axis=0).astype(jnp.bfloat16)
    places = iota((capacity, pairs), 0)
    for s in range(lists):
        chosen = jnp.where(slot[s : s + 1, :] == places, 1.0, 0.0).astype(jnp.bfloat16)
        got = row_dot(packed, chosen).astype(jnp.int32)
        high, low, which, pair = [got[i * lists + s : i * lists + s + 1, :] for i in range(4)]
        asked, j = s // chips, s % chips
        if asked < 4:
            request_refs[j][asked : asked + 1, :] = 2 * (high * 256 + low)
        if asked in (0, 2, 4, 5):
            at = j if asked < 4 else chips + j
            bag_ref = near_ref if asked in (0, 4) else far_ref
            bag_ref[at : at + 1, :] = (which - 1) * pairs + pair


def widen_kernel(table_ref, wide_ref):
    width = table_ref.shape[1]
    step = 128

    def widen(i, carry):
        start = pl.multiple_of(i * step, step)
        part = table_ref[pl.ds(start, step), :].astype(jnp.float32)
        wide_ref[pl.ds(2 * start, step, stride=2), :] = part[:, : width // 2]
        wide_ref[pl.ds(2 * start + 1, step, stride=2), :] = part[:, width // 2 :]
        return carry

    lax.fori_loop(0, table_ref.shape[0] // step, widen, 0)


def gather_kernel(chips, askers, *refs):
    wanted, wide_ref, refs = refs[:chips], refs[chips], refs[chips + 1 :]
    outs, (index_ref, stage, sems) = refs[: len(askers)], refs[len(askers) :]
    _, capacity, width = outs[0].shape
    group = 16
    copies = [
        pltpu.make_async_copy(wanted[chips - 1 - j], index_ref.at[j], sems.at[j])
        for j in range(chips)
    ]
    for copy in copies:
        copy.start()
    for copy in copies:
        copy.wait()
    for asker, out_ref in zip(askers, outs):
        for j in range(chips):
            for base in range(0, capacity, group):
                found = [
                    wide_ref[pl.ds(index_ref[j, asker, base + i], 2), :] for i in range(group)
                ]
                for i in range(group):
                    stage[pl.ds(2 * (base + i), 2), :] = found[i]
            for part in range(2):
                values = stage[pl.ds(part, capacity, stride=2), :]
                out_ref[j, :, part * (width // 2) : (part + 1) * (width // 2)] = values.astype(
                    jnp.bfloat16
                )


def pack_kernel(chips, same_ref, swapped_ref, *out_refs):
    for out_ref, j in zip(out_refs, range(chips - 1, 0, -1)):
        out_ref[0] = same_ref[j]
        out_ref[1] = swapped_ref[j]


def bag_sums(bag_ref, rows, bags, first):
    total = None
    for at, values in enumerate(rows):
        chosen = bag_ref[at : at + 1, :] == first + iota((bags, bag_ref.shape[1]), 0)
        part = dot(jnp.where(chosen, 1.0, 0.0).astype(jnp.bfloat16), values)
        total = part if total is None else total + part
    return total


def lists_of(order, same_ref, swapped_ref, message_refs):
    chips = len(order) + 1
    return [
        own_ref[0] if j == 0 else message_refs[order.index(j)][f]
        for f, own_ref in enumerate((same_ref, swapped_ref))
        for j in range(chips)
    ]


def sum_kernel(order, kind, bag_ref, same_ref, swapped_ref, *refs):
    out_ref = refs[-1]
    pairs = out_ref.shape[0]
    rows = lists_of(order, same_ref, swapped_ref, refs[:-1])
    out_ref[...] = bag_sums(bag_ref, rows, pairs, kind * pairs).astype(out_ref.dtype)


def item_kernel(order, bag_ref, far_ref, same_ref, swapped_ref, *refs):
    messages, (unit_ref, scale_ref, bf_ref) = refs[:-3], refs[-3:]
    pairs = bf_ref.shape[0]
    rows = lists_of(order, same_ref, swapped_ref, messages)
    total = bag_sums(bag_ref, rows, pairs, pairs) + far_ref[...].astype(jnp.float32)
    unit, scale = unit_rows(total)
    unit_ref[...] = unit
    scale_ref[...] = scale
    bf_ref[...] = unit.astype(jnp.bfloat16)


def tower_kernel(
    near_ref, far_ref, first_ref, second_ref, unit_ref, scale_ref, bf_ref, slope_ref
):
    query_in = (near_ref[...] + far_ref[...].astype(jnp.float32)).astype(jnp.bfloat16)
    query_in = (0.5 * query_in.astype(jnp.float32)).astype(jnp.bfloat16)
    step = 1024
    total = None
    for at in range(0, first_ref.shape[1], step):
        pre = dot(query_in, first_ref[:, at : at + step])
        turn = jnp.tanh(pre)
        hidden = pre + pre * turn
        turn = 0.5 * turn
        slope_ref[:, at : at + step] = (0.5 + turn) + hidden * (0.5 - turn)
        part = dot(hidden.astype(jnp.bfloat16), second_ref[at : at + step, :])
        total = part if total is None else total + part
    unit, scale = unit_rows(total)
    unit_ref[...] = unit
    scale_ref[...] = scale
    bf_ref[...] = unit.astype(jnp.bfloat16)


def group_exps(query, item):
    return jnp.exp(INV_TEMP * row_dot(query, item))


def row_sums(values):
    return jnp.sum(values, axis=1, keepdims=True)


def query_grad_kernel(blocks, *refs):
    query_ref, items, refs = refs[0], refs[1 : 1 + blocks], refs[1 + blocks :]
    first_ref, second_ref, slope_ref, unit_ref, scale_ref, loss_ref, grad_ref, item_sum_ref = refs
    query = query_ref[...]
    kept = [group_exps(query, item[...]) for item in items[:2]]
    total = sum(row_sums(exps) for exps in kept)
    for item in items[2:]:
        total = total + row_sums(group_exps(query, item[...]))
    inverse = 1.0 / total
    query_sum = jnp.zeros(query.shape, jnp.float32)
    for j, item in enumerate(items):
        exps = kept[j] if j < 2 else group_exps(query, item[...])
        probs = (exps * inverse).astype(jnp.bfloat16)
        query_sum = query_sum + dot(probs, item[...])
        if j == 0:
            item_sum_ref[...] = col_dot(probs, query)
    wide_item = items[0][...].astype(jnp.float32)
    own = INV_TEMP * row_sums(query.astype(jnp.float32) * wide_item)
    loss_ref[...] = (jnp.log(total) - own).T
    out_grad = unit_backward(
        INV_TEMP * (query_sum - wide_item), unit_ref[...], scale_ref[...]
    ).astype(jnp.bfloat16)
    step = 1024
    total = None
    for at in range(0, first_ref.shape[1], step):
        back = row_dot(out_grad, second_ref[at : at + step, :])
        hidden_grad = (back * slope_ref[:, at : at + step]).astype(jnp.bfloat16)
        part = row_dot(hidden_grad, first_ref[:, at : at + step])
        total = part if total is None else total + part
    grad_ref[...] = total


def item_grad_kernel(blocks, *refs):
    queries, items, refs = refs[:blocks], refs[blocks : 2 * blocks], refs[2 * blocks :]
    item_sum_ref, unit_ref, scale_ref, grad_ref = refs
    item_sum = item_sum_ref[...]
    for i in range(1, blocks):
        query = queries[i][...]
        own_exps = group_exps(query, items[0][...])
        total = row_sums(own_exps)
        for j in range(1, blocks):
            total = total + row_sums(group_exps(query, items[j][...]))
        item_sum = item_sum + col_dot((own_exps * (1.0 / total)).astype(jnp.bfloat16), query)
    grad_ref[...] = unit_backward(
        INV_TEMP * (item_sum - queries[0][...].astype(jnp.float32)), unit_ref[...], scale_ref[...]
    )


def rotated(shard, axis, by):
    count = lax.axis_size(axis)
    return lax.ppermute(shard, axis, [(i, (i + by) % count) for i in range(count)])


def struct(shape, dtype):
    return jax.ShapeDtypeStruct(shape, dtype)


def local(id_table, w_first, w_second, owner_ids, row_ids):
    pairs, bags = owner_ids.shape
    shards = lax.axis_size("table")
    blocks = lax.axis_size("blk")
    width = id_table.shape[1]
    hidden_units = w_first.shape[1]
    capacity = min(pairs, 3 * pairs * bags // (2 * shards))
    bf, f32 = jnp.bfloat16, jnp.float32

    half = shards // 2
    chips = half // 2
    power = chips & (chips - 1) == 0

    def relative(chip, j):
        return chip ^ j if power else (chip + j) % chips

    def to_chip(values, j, flip=0):
        if j == 0 and flip == 0:
            return values
        route = [
            (t, t // half * half + relative(t % half // 2, j) * 2 + (t % 2 ^ flip))
            for t in range(shards)
        ]
        return lax.ppermute(values, "table", route)

    def to_mirror(values):
        return lax.ppermute(values, "table", [(t, (t + half) % shards) for t in range(shards)])

    code = owner_ids * id_table.shape[0] + row_ids
    mirror_code = to_mirror(code)
    codes = [code, to_chip(code, 0, 1), mirror_code, to_chip(mirror_code, 0, 1)]
    wide = pl.pallas_call(
        widen_kernel,
        out_shape=struct((2 * id_table.shape[0], width // 2), f32),
        compiler_params=params(8),
        name="widen",
    )(id_table)
    near_bags, far_bags, *requests = pl.pallas_call(
        functools.partial(route_kernel, relative, id_table.shape[0]),
        out_shape=[struct((half, capacity), jnp.int32)] * 2
        + [struct((4, capacity), jnp.int32)] * chips,
        compiler_params=params(4),
        name="route",
    )(*[c.T for c in codes])
    wanted = [to_chip(requests[j], j) for j in reversed(range(chips))][::-1]

    def gather(askers):
        return pl.pallas_call(
            functools.partial(gather_kernel, chips, askers),
            in_specs=[pl.BlockSpec(memory_space=pl.ANY)] * chips
            + [pl.BlockSpec(memory_space=pltpu.VMEM)],
            out_shape=[struct((chips, capacity, width), bf)] * len(askers),
            scratch_shapes=[
                pltpu.SMEM((chips, 4, capacity), jnp.int32),
                pltpu.VMEM((2 * capacity, width // 2), f32),
                pltpu.SemaphoreType.DMA((chips,)),
            ],
            compiler_params=params(8),
            name="gather",
        )(*wanted[::-1], wide)

    order = list(range(chips - 1, 0, -1))

    def answered(same, swapped):
        messages = pl.pallas_call(
            functools.partial(pack_kernel, chips),
            out_shape=[struct((2, capacity, width), bf)] * (chips - 1),
            compiler_params=params(8),
            name="pack",
        )(same, swapped)
        arrived = []
        for j in order:
            back = j if power else (chips - j) % chips
            arrived.append(to_chip(messages[chips - 1 - back], back))
        return (same, swapped, *arrived), messages

    far_other, near_other = [to_chip(rows, 0, 1) for rows in gather((3, 1))]
    far_same, near_same = gather((2, 0))
    far_rows, _ = answered(far_same, far_other)
    near_rows, near_messages = answered(near_same, near_other)
    far_bags, _ = lax.optimization_barrier((far_bags, near_messages[-1]))

    def sums(kind, bags, rows, dtype):
        return pl.pallas_call(
            functools.partial(sum_kernel, order, kind),
            out_shape=struct((pairs, width), dtype),
            compiler_params=params(8),
            name="item_sums" if kind else "query_sums",
        )(bags, *rows)

    far_item = sums(1, far_bags, far_rows, bf)
    far_bags, _ = lax.optimization_barrier((far_bags, far_item))
    far_query = to_mirror(sums(0, far_bags, far_rows, bf))
    far_item = to_mirror(far_item)
    item_unit, item_scale, item_bf = pl.pallas_call(
        functools.partial(item_kernel, order),
        out_shape=[
            struct((pairs, width), f32),
            struct((pairs, 1), f32),
            struct((pairs, width), bf),
        ],
        compiler_params=params(8),
        name="items",
    )(near_bags, far_item, *near_rows)
    near_bags, _ = lax.optimization_barrier((near_bags, item_bf))
    near_query = sums(0, near_bags, near_rows, f32)
    items = [item_bf] + [rotated(item_bf, "blk", by) for by in range(1, blocks)]
    query_unit, query_scale, query_bf, slope = pl.pallas_call(
        tower_kernel,
        out_shape=[
            struct((pairs, width), f32),
            struct((pairs, 1), f32),
            struct((pairs, width), bf),
            struct((pairs, hidden_units), f32),
        ],
        compiler_params=params(12),
        name="tower",
    )(near_query, far_query, w_first, w_second)
    queries = [query_bf] + [rotated(query_bf, "blk", by) for by in range(1, blocks)]
    loss, query_grad, own_sum = pl.pallas_call(
        functools.partial(query_grad_kernel, blocks),
        out_shape=[
            struct((1, pairs), f32),
            struct((pairs, width), f32),
            struct((pairs, width), f32),
        ],
        compiler_params=params(12),
        name="query_grads",
    )(query_bf, *items, w_first, w_second, slope, query_unit, query_scale)
    item_grad = pl.pallas_call(
        functools.partial(item_grad_kernel, blocks),
        out_shape=struct((pairs, width), f32),
        compiler_params=params(12),
        name="item_grads",
    )(*queries, *items, own_sum, item_unit, item_scale)
    return loss.reshape(pairs), item_grad, query_grad


def solution(mesh):
    placed = (P("table", None), P(), P(), P(("blk", "table"), None), P(("blk", "table"), None))
    return jax.shard_map(
        local,
        mesh=mesh,
        in_specs=placed,
        out_specs=(P(("blk", "table")), P(("blk", "table"), None), P(("blk", "table"), None)),
        check_vma=False,
    )
```

```python
import functools

import jax
import jax.numpy as jnp
from jax import lax
from jax.experimental import pallas as pl
from jax.experimental.pallas import tpu as pltpu
from jax.sharding import PartitionSpec as P

EPS = 1e-06
INV_TEMP = 20.0


def params(mebibytes):
    return pltpu.CompilerParams(vmem_limit_bytes=mebibytes * 1024 * 1024)


def iota(shape, dim):
    return lax.broadcasted_iota(jnp.int32, shape, dim)


def row_dot(left, right):
    return lax.dot_general(
        left, right, (((1,), (1,)), ((), ())), preferred_element_type=jnp.float32
    )


def col_dot(left, right):
    return lax.dot_general(
        left, right, (((0,), (0,)), ((), ())), preferred_element_type=jnp.float32
    )


def dot(left, right):
    return jnp.dot(left, right, preferred_element_type=jnp.float32)


def unit_rows(vectors):
    scale = lax.rsqrt(jnp.sum(vectors * vectors, axis=-1, keepdims=True) + EPS)
    return vectors * scale, scale


def unit_backward(grad, unit, scale):
    return scale * (grad - unit * jnp.sum(unit * grad, axis=-1, keepdims=True))


def route_kernel(relative, rows_dev, *refs):
    codes, near_ref, far_ref, request_refs = refs[:4], refs[5], refs[6], refs[7:]
    chips = len(request_refs)
    bags, pairs = codes[0].shape
    capacity = near_ref.shape[1]
    lists = 6 * chips
    place = lax.axis_index("table")
    half = 2 * chips
    list_of = iota((lists, pairs), 0)
    chip = relative(place % half // 2, list_of % chips)
    asker = list_of // chips
    core = jnp.where(asker < 4, place % 2, 1 - place % 2)
    start = (place // half * half + chip * 2 + core) * rows_dev
    named = jnp.zeros((lists, pairs), jnp.float32)
    rows = jnp.zeros((lists, pairs), jnp.int32)
    kind = jnp.zeros((lists, pairs), jnp.int32)
    for k in range(bags):
        code = codes[0][k : k + 1, :]
        for r, at in ((1, 1), (2, 2), (3, 3), (5, 2)):
            code = jnp.where(asker == r, codes[at][k : k + 1, :], code)
        row = code - start
        hit = (row >= 0) & (row < rows_dev)
        named = jnp.where(hit, 1.0, named)
        rows = jnp.where(hit, row, rows)
        kind = jnp.where(hit, 1 if k < bags // 2 else 2, kind)
    before = jnp.where(iota((pairs, pairs), 0) < iota((pairs, pairs), 1), 1.0, 0.0)
    slot = dot(named.astype(jnp.bfloat16), before.astype(jnp.bfloat16)).astype(jnp.int32)
    slot = jnp.where(named > 0.0, slot, -1)
    digits = [rows // 256, rows % 256, kind, iota((lists, pairs), 1)]
    packed = jnp.concatenate([d.astype(jnp.float32) for d in digits], axis=0).astype(jnp.bfloat16)
    places = iota((capacity, pairs), 0)
    for s in range(lists):
        chosen = jnp.where(slot[s : s + 1, :] == places, 1.0, 0.0).astype(jnp.bfloat16)
        got = row_dot(packed, chosen).astype(jnp.int32)
        high, low, which, pair = [got[i * lists + s : i * lists + s + 1, :] for i in range(4)]
        asked, j = s // chips, s % chips
        if asked < 4:
            request_refs[j][asked : asked + 1, :] = 2 * (high * 256 + low)
        if asked in (0, 2, 4, 5):
            at = j if asked < 4 else chips + j
            bag_ref = near_ref if asked in (0, 4) else far_ref
            bag_ref[at : at + 1, :] = (which - 1) * pairs + pair


def touch_kernel(table_hbm, out_ref, rows_ref, sem):
    copy = pltpu.make_async_copy(table_hbm.at[pl.ds(0, rows_ref.shape[0]), :], rows_ref, sem)
    copy.start()
    copy.wait()
    out_ref[...] = rows_ref[...].astype(jnp.float32)


def widen_kernel(table_ref, wide_ref):
    width = table_ref.shape[1]
    step = 128

    def widen(i, carry):
        start = pl.multiple_of(i * step, step)
        part = table_ref[pl.ds(start, step), :].astype(jnp.float32)
        wide_ref[pl.ds(2 * start, step, stride=2), :] = part[:, : width // 2]
        wide_ref[pl.ds(2 * start + 1, step, stride=2), :] = part[:, width // 2 :]
        return carry

    lax.fori_loop(0, table_ref.shape[0] // step, widen, 0)


def gather_kernel(chips, askers, *refs):
    wanted, wide_ref, refs = refs[:chips], refs[chips], refs[chips + 1 :]
    outs, (index_ref, stage, sems) = refs[: len(askers)], refs[len(askers) :]
    _, capacity, width = outs[0].shape
    group = 16
    copies = [
        pltpu.make_async_copy(wanted[chips - 1 - j], index_ref.at[j], sems.at[j])
        for j in range(chips)
    ]
    for copy in copies:
        copy.start()
    for copy in copies:
        copy.wait()
    for asker, out_ref in zip(askers, outs):
        for j in range(chips):
            for base in range(0, capacity, group):
                found = [
                    wide_ref[pl.ds(index_ref[j, asker, base + i], 2), :] for i in range(group)
                ]
                for i in range(group):
                    stage[pl.ds(2 * (base + i), 2), :] = found[i]
            for part in range(2):
                values = stage[pl.ds(part, capacity, stride=2), :]
                out_ref[j, :, part * (width // 2) : (part + 1) * (width // 2)] = values.astype(
                    jnp.bfloat16
                )


def pack_kernel(chips, same_ref, swapped_ref, *out_refs):
    for out_ref, j in zip(out_refs, range(chips - 1, 0, -1)):
        out_ref[0] = same_ref[j]
        out_ref[1] = swapped_ref[j]


def bag_sums(bag_ref, rows, bags, first):
    total = None
    for at, values in enumerate(rows):
        chosen = bag_ref[at : at + 1, :] == first + iota((bags, bag_ref.shape[1]), 0)
        part = dot(jnp.where(chosen, 1.0, 0.0).astype(jnp.bfloat16), values)
        total = part if total is None else total + part
    return total


def lists_of(order, same_ref, swapped_ref, message_refs):
    chips = len(order) + 1
    return [
        own_ref[0] if j == 0 else message_refs[order.index(j)][f]
        for f, own_ref in enumerate((same_ref, swapped_ref))
        for j in range(chips)
    ]


def sum_kernel(order, kind, bag_ref, same_ref, swapped_ref, *refs):
    out_ref = refs[-1]
    pairs = out_ref.shape[0]
    rows = lists_of(order, same_ref, swapped_ref, refs[:-1])
    out_ref[...] = bag_sums(bag_ref, rows, pairs, kind * pairs).astype(out_ref.dtype)


def item_kernel(order, bag_ref, far_ref, same_ref, swapped_ref, *refs):
    messages, (unit_ref, scale_ref, bf_ref) = refs[:-3], refs[-3:]
    pairs = bf_ref.shape[0]
    rows = lists_of(order, same_ref, swapped_ref, messages)
    total = bag_sums(bag_ref, rows, pairs, pairs) + far_ref[...].astype(jnp.float32)
    unit, scale = unit_rows(total)
    unit_ref[...] = unit
    scale_ref[...] = scale
    bf_ref[...] = unit.astype(jnp.bfloat16)


def tower_kernel(
    near_ref, far_ref, first_ref, second_ref, unit_ref, scale_ref, bf_ref, slope_ref
):
    query_in = (near_ref[...] + far_ref[...].astype(jnp.float32)).astype(jnp.bfloat16)
    query_in = (0.5 * query_in.astype(jnp.float32)).astype(jnp.bfloat16)
    step = 1024
    total = None
    for at in range(0, first_ref.shape[1], step):
        pre = dot(query_in, first_ref[:, at : at + step])
        turn = jnp.tanh(pre)
        hidden = pre + pre * turn
        turn = 0.5 * turn
        slope_ref[:, at : at + step] = (0.5 + turn) + hidden * (0.5 - turn)
        part = dot(hidden.astype(jnp.bfloat16), second_ref[at : at + step, :])
        total = part if total is None else total + part
    unit, scale = unit_rows(total)
    unit_ref[...] = unit
    scale_ref[...] = scale
    bf_ref[...] = unit.astype(jnp.bfloat16)


def group_exps(query, item):
    return jnp.exp(INV_TEMP * row_dot(query, item))


def row_sums(values):
    return jnp.sum(values, axis=1, keepdims=True)


def query_grad_kernel(blocks, *refs):
    query_ref, items, refs = refs[0], refs[1 : 1 + blocks], refs[1 + blocks :]
    first_ref, second_ref, slope_ref, unit_ref, scale_ref, loss_ref, grad_ref, item_sum_ref = refs
    query = query_ref[...]
    kept = [group_exps(query, item[...]) for item in items[:2]]
    total = sum(row_sums(exps) for exps in kept)
    for item in items[2:]:
        total = total + row_sums(group_exps(query, item[...]))
    inverse = 1.0 / total
    query_sum = jnp.zeros(query.shape, jnp.float32)
    for j, item in enumerate(items):
        exps = kept[j] if j < 2 else group_exps(query, item[...])
        probs = (exps * inverse).astype(jnp.bfloat16)
        query_sum = query_sum + dot(probs, item[...])
        if j == 0:
            item_sum_ref[...] = col_dot(probs, query)
    wide_item = items[0][...].astype(jnp.float32)
    own = INV_TEMP * row_sums(query.astype(jnp.float32) * wide_item)
    loss_ref[...] = (jnp.log(total) - own).T
    out_grad = unit_backward(
        INV_TEMP * (query_sum - wide_item), unit_ref[...], scale_ref[...]
    ).astype(jnp.bfloat16)
    step = 1024
    total = None
    for at in range(0, first_ref.shape[1], step):
        back = row_dot(out_grad, second_ref[at : at + step, :])
        hidden_grad = (back * slope_ref[:, at : at + step]).astype(jnp.bfloat16)
        part = row_dot(hidden_grad, first_ref[:, at : at + step])
        total = part if total is None else total + part
    grad_ref[...] = total


def item_grad_kernel(blocks, *refs):
    queries, items, refs = refs[:blocks], refs[blocks : 2 * blocks], refs[2 * blocks :]
    item_sum_ref, unit_ref, scale_ref, loss_ref, query_grad_ref, grad_ref, *outs, sems = refs
    copies = [
        pltpu.make_async_copy(given, out, sems.at[i])
        for i, (given, out) in enumerate(zip((loss_ref, query_grad_ref), outs))
    ]
    for copy in copies:
        copy.start()
    item_sum = item_sum_ref[...]
    for i in range(1, blocks):
        query = queries[i][...]
        own_exps = group_exps(query, items[0][...])
        total = row_sums(own_exps)
        for j in range(1, blocks):
            total = total + row_sums(group_exps(query, items[j][...]))
        item_sum = item_sum + col_dot((own_exps * (1.0 / total)).astype(jnp.bfloat16), query)
    grad_ref[...] = unit_backward(
        INV_TEMP * (item_sum - queries[0][...].astype(jnp.float32)), unit_ref[...], scale_ref[...]
    )
    for copy in copies:
        copy.wait()


def rotated(shard, axis, by):
    count = lax.axis_size(axis)
    return lax.ppermute(shard, axis, [(i, (i + by) % count) for i in range(count)])


def struct(shape, dtype):
    return jax.ShapeDtypeStruct(shape, dtype)


def local(id_table, w_first, w_second, owner_ids, row_ids):
    pairs, bags = owner_ids.shape
    shards = lax.axis_size("table")
    blocks = lax.axis_size("blk")
    width = id_table.shape[1]
    hidden_units = w_first.shape[1]
    capacity = min(pairs, 3 * pairs * bags // (2 * shards))
    bf, f32 = jnp.bfloat16, jnp.float32

    half = shards // 2
    chips = half // 2
    power = chips & (chips - 1) == 0

    def relative(chip, j):
        return chip ^ j if power else (chip + j) % chips

    def to_chip(values, j, flip=0):
        if j == 0 and flip == 0:
            return values
        route = [
            (t, t // half * half + relative(t % half // 2, j) * 2 + (t % 2 ^ flip))
            for t in range(shards)
        ]
        return lax.ppermute(values, "table", route)

    def to_mirror(values):
        return lax.ppermute(values, "table", [(t, (t + half) % shards) for t in range(shards)])

    code = owner_ids * id_table.shape[0] + row_ids
    mirror_code = to_mirror(code)
    codes = [code, to_chip(code, 0, 1), mirror_code, to_chip(mirror_code, 0, 1)]
    touched = pl.pallas_call(
        touch_kernel,
        in_specs=[pl.BlockSpec(memory_space=pl.ANY)],
        out_shape=struct((16, width), f32),
        scratch_shapes=[pltpu.VMEM((16, width), bf), pltpu.SemaphoreType.DMA(())],
        compiler_params=params(52),
        name="touch",
    )(id_table)
    wide = pl.pallas_call(
        widen_kernel,
        out_shape=struct((2 * id_table.shape[0], width // 2), f32),
        compiler_params=params(8),
        name="widen",
    )(id_table)
    near_bags, far_bags, *requests = pl.pallas_call(
        functools.partial(route_kernel, relative, id_table.shape[0]),
        out_shape=[struct((half, capacity), jnp.int32)] * 2
        + [struct((4, capacity), jnp.int32)] * chips,
        compiler_params=params(4),
        name="route",
    )(*[c.T for c in codes], touched)
    wanted = [to_chip(requests[j], j) for j in reversed(range(chips))][::-1]

    def gather(askers):
        return pl.pallas_call(
            functools.partial(gather_kernel, chips, askers),
            in_specs=[pl.BlockSpec(memory_space=pl.ANY)] * chips
            + [pl.BlockSpec(memory_space=pltpu.VMEM)],
            out_shape=[struct((chips, capacity, width), bf)] * len(askers),
            scratch_shapes=[
                pltpu.SMEM((chips, 4, capacity), jnp.int32),
                pltpu.VMEM((2 * capacity, width // 2), f32),
                pltpu.SemaphoreType.DMA((chips,)),
            ],
            compiler_params=params(8),
            name="gather",
        )(*wanted[::-1], wide)

    order = list(range(chips - 1, 0, -1))

    def answered(same, swapped):
        messages = pl.pallas_call(
            functools.partial(pack_kernel, chips),
            out_shape=[struct((2, capacity, width), bf)] * (chips - 1),
            compiler_params=params(8),
            name="pack",
        )(same, swapped)
        arrived = []
        for j in order:
            back = j if power else (chips - j) % chips
            arrived.append(to_chip(messages[chips - 1 - back], back))
        return (same, swapped, *arrived), messages

    far_other, near_other = [to_chip(rows, 0, 1) for rows in gather((3, 1))]
    far_same, near_same = gather((2, 0))
    far_rows, _ = answered(far_same, far_other)
    near_rows, near_messages = answered(near_same, near_other)
    far_bags, _ = lax.optimization_barrier((far_bags, near_messages[-1]))

    def sums(kind, bags, rows, dtype):
        return pl.pallas_call(
            functools.partial(sum_kernel, order, kind),
            out_shape=struct((pairs, width), dtype),
            compiler_params=params(8),
            name="item_sums" if kind else "query_sums",
        )(bags, *rows)

    far_item = sums(1, far_bags, far_rows, bf)
    far_bags, _ = lax.optimization_barrier((far_bags, far_item))
    far_query = to_mirror(sums(0, far_bags, far_rows, bf))
    far_item = to_mirror(far_item)
    item_unit, item_scale, item_bf = pl.pallas_call(
        functools.partial(item_kernel, order),
        out_shape=[
            struct((pairs, width), f32),
            struct((pairs, 1), f32),
            struct((pairs, width), bf),
        ],
        compiler_params=params(8),
        name="items",
    )(near_bags, far_item, *near_rows)
    near_bags, _ = lax.optimization_barrier((near_bags, item_bf))
    near_query = sums(0, near_bags, near_rows, f32)
    items = [item_bf] + [rotated(item_bf, "blk", by) for by in range(1, blocks)]
    query_unit, query_scale, query_bf, slope = pl.pallas_call(
        tower_kernel,
        out_shape=[
            struct((pairs, width), f32),
            struct((pairs, 1), f32),
            struct((pairs, width), bf),
            struct((pairs, hidden_units), f32),
        ],
        compiler_params=params(12),
        name="tower",
    )(near_query, far_query, w_first, w_second)
    queries = [query_bf] + [rotated(query_bf, "blk", by) for by in range(1, blocks)]
    loss, query_grad, own_sum = pl.pallas_call(
        functools.partial(query_grad_kernel, blocks),
        out_shape=[
            struct((1, pairs), f32),
            struct((pairs, width), f32),
            struct((pairs, width), f32),
        ],
        compiler_params=params(12),
        name="query_grads",
    )(query_bf, *items, w_first, w_second, slope, query_unit, query_scale)
    queries, loss = lax.optimization_barrier((queries, loss))
    in_vmem, anywhere = pl.BlockSpec(memory_space=pltpu.VMEM), pl.BlockSpec(memory_space=pl.ANY)
    item_grad, loss, query_grad = pl.pallas_call(
        functools.partial(item_grad_kernel, blocks),
        in_specs=[in_vmem] * (2 * blocks + 3) + [anywhere] * 2,
        out_specs=[in_vmem, anywhere, anywhere],
        out_shape=[
            struct((pairs, width), f32),
            struct((1, pairs), f32),
            struct((pairs, width), f32),
        ],
        scratch_shapes=[pltpu.SemaphoreType.DMA((2,))],
        compiler_params=params(12),
        name="item_grads",
    )(*queries, *items, own_sum, item_unit, item_scale, loss, query_grad)
    return loss.reshape(pairs), item_grad, query_grad


def solution(mesh):
    placed = (P("table", None), P(), P(), P(("blk", "table"), None), P(("blk", "table"), None))
    return jax.shard_map(
        local,
        mesh=mesh,
        in_specs=placed,
        out_specs=(P(("blk", "table")), P(("blk", "table"), None), P(("blk", "table"), None)),
        check_vma=False,
    )
```

```python
import functools

import jax
import jax.numpy as jnp
from jax import lax
from jax.experimental import pallas as pl
from jax.experimental.pallas import tpu as pltpu
from jax.sharding import PartitionSpec as P

EPS = 1e-06
INV_TEMP = 20.0


def params(mebibytes):
    return pltpu.CompilerParams(vmem_limit_bytes=mebibytes * 1024 * 1024)


def iota(shape, dim):
    return lax.broadcasted_iota(jnp.int32, shape, dim)


def row_dot(left, right):
    return lax.dot_general(
        left, right, (((1,), (1,)), ((), ())), preferred_element_type=jnp.float32
    )


def col_dot(left, right):
    return lax.dot_general(
        left, right, (((0,), (0,)), ((), ())), preferred_element_type=jnp.float32
    )


def dot(left, right):
    return jnp.dot(left, right, preferred_element_type=jnp.float32)


def unit_rows(vectors):
    scale = lax.rsqrt(jnp.sum(vectors * vectors, axis=-1, keepdims=True) + EPS)
    return vectors * scale, scale


def unit_backward(grad, unit, scale):
    return scale * (grad - unit * jnp.sum(unit * grad, axis=-1, keepdims=True))


def packed_lists(relative, rows_dev, askers, codes, chips, capacity):
    bags, pairs = codes[0].shape
    lists = len(askers) * chips
    place = lax.axis_index("table")
    half = 2 * chips
    list_of = iota((lists, pairs), 0)
    chip = relative(place % half // 2, list_of % chips)
    asker = list_of // chips
    core = place % 2
    for at, name in enumerate(askers):
        if name >= 4:
            core = jnp.where(asker == at, 1 - place % 2, core)
    start = (place // half * half + chip * 2 + core) * rows_dev
    named = jnp.zeros((lists, pairs), jnp.float32)
    rows = jnp.zeros((lists, pairs), jnp.int32)
    kind = jnp.zeros((lists, pairs), jnp.int32)
    for k in range(bags):
        code = codes[(0, 1, 2, 3, 0, 2)[askers[0]]][k : k + 1, :]
        for at, name in enumerate(askers[1:], 1):
            code = jnp.where(asker == at, codes[(0, 1, 2, 3, 0, 2)[name]][k : k + 1, :], code)
        row = code - start
        hit = (row >= 0) & (row < rows_dev)
        named = jnp.where(hit, 1.0, named)
        rows = jnp.where(hit, row, rows)
        kind = jnp.where(hit, 1 if k < bags // 2 else 2, kind)
    before = jnp.where(iota((pairs, pairs), 0) < iota((pairs, pairs), 1), 1.0, 0.0)
    slot = dot(named.astype(jnp.bfloat16), before.astype(jnp.bfloat16)).astype(jnp.int32)
    slot = jnp.where(named > 0.0, slot, -1)
    digits = [rows // 256, rows % 256, kind, iota((lists, pairs), 1)]
    packed = jnp.concatenate([d.astype(jnp.float32) for d in digits], axis=0).astype(jnp.bfloat16)
    places = iota((capacity, pairs), 0)
    for s in range(lists):
        chosen = jnp.where(slot[s : s + 1, :] == places, 1.0, 0.0).astype(jnp.bfloat16)
        got = row_dot(packed, chosen).astype(jnp.int32)
        high, low, which, pair = [got[i * lists + s : i * lists + s + 1, :] for i in range(4)]
        yield s // chips, s % chips, high * 256 + low, which, pair


def route_kernel(relative, rows_dev, *refs):
    codes, requests = refs[:4], refs[5:]
    capacity = requests[0].shape[1]
    lists = packed_lists(relative, rows_dev, (0, 1, 2, 3), codes, len(requests), capacity)
    for at, j, row, _, _ in lists:
        requests[j][at : at + 1, :] = 2 * row


def bag_kernel(relative, rows_dev, *refs):
    codes, outs = refs[:4], refs[4:]
    half, capacity = outs[0].shape
    pairs = codes[0].shape[1]
    chips = half // 2
    lists = packed_lists(relative, rows_dev, (0, 4, 2, 5), codes, chips, capacity)
    for at, j, _, which, pair in lists:
        place = at % 2 * chips + j
        outs[at // 2][place : place + 1, :] = (which - 1) * pairs + pair


def touch_kernel(table_hbm, out_ref, rows_ref, sem):
    copy = pltpu.make_async_copy(table_hbm.at[pl.ds(0, rows_ref.shape[0]), :], rows_ref, sem)
    copy.start()
    copy.wait()
    out_ref[...] = rows_ref[...].astype(jnp.float32)


def widen_kernel(table_ref, wide_ref):
    width = table_ref.shape[1]
    step = 128

    def widen(i, carry):
        start = pl.multiple_of(i * step, step)
        part = table_ref[pl.ds(start, step), :].astype(jnp.float32)
        wide_ref[pl.ds(2 * start, step, stride=2), :] = part[:, : width // 2]
        wide_ref[pl.ds(2 * start + 1, step, stride=2), :] = part[:, width // 2 :]
        return carry

    lax.fori_loop(0, table_ref.shape[0] // step, widen, 0)


def gather_kernel(chips, askers, *refs):
    wanted, wide_ref, refs = refs[:chips], refs[chips], refs[chips + 1 :]
    outs, (index_ref, stage, sems) = refs[: len(askers)], refs[len(askers) :]
    _, capacity, width = outs[0].shape
    group = 16
    copies = [
        pltpu.make_async_copy(wanted[chips - 1 - j], index_ref.at[j], sems.at[j])
        for j in range(chips)
    ]
    for copy in copies:
        copy.start()
    for copy in copies:
        copy.wait()
    for asker, out_ref in zip(askers, outs):
        for j in range(chips):
            for base in range(0, capacity, group):
                found = [
                    wide_ref[pl.ds(index_ref[j, asker, base + i], 2), :] for i in range(group)
                ]
                for i in range(group):
                    stage[pl.ds(2 * (base + i), 2), :] = found[i]
            for part in range(2):
                values = stage[pl.ds(part, capacity, stride=2), :]
                out_ref[j, :, part * (width // 2) : (part + 1) * (width // 2)] = values.astype(
                    jnp.bfloat16
                )


def pack_kernel(chips, same_ref, swapped_ref, *out_refs):
    for out_ref, j in zip(out_refs, range(chips - 1, 0, -1)):
        out_ref[0] = same_ref[j]
        out_ref[1] = swapped_ref[j]


def bag_sums(bag_ref, rows, bags, first):
    total = None
    for at, values in enumerate(rows):
        chosen = bag_ref[at : at + 1, :] == first + iota((bags, bag_ref.shape[1]), 0)
        part = dot(jnp.where(chosen, 1.0, 0.0).astype(jnp.bfloat16), values)
        total = part if total is None else total + part
    return total


def lists_of(order, same_ref, swapped_ref, message_refs):
    chips = len(order) + 1
    return [
        own_ref[0] if j == 0 else message_refs[order.index(j)][f]
        for f, own_ref in enumerate((same_ref, swapped_ref))
        for j in range(chips)
    ]


def sum_kernel(order, kind, bag_ref, same_ref, swapped_ref, *refs):
    out_ref = refs[-1]
    pairs = out_ref.shape[0]
    rows = lists_of(order, same_ref, swapped_ref, refs[:-1])
    out_ref[...] = bag_sums(bag_ref, rows, pairs, kind * pairs).astype(out_ref.dtype)


def item_kernel(order, bag_ref, far_ref, same_ref, swapped_ref, *refs):
    messages, (unit_ref, scale_ref, bf_ref) = refs[:-3], refs[-3:]
    pairs = bf_ref.shape[0]
    rows = lists_of(order, same_ref, swapped_ref, messages)
    total = bag_sums(bag_ref, rows, pairs, pairs) + far_ref[...].astype(jnp.float32)
    unit, scale = unit_rows(total)
    unit_ref[...] = unit
    scale_ref[...] = scale
    bf_ref[...] = unit.astype(jnp.bfloat16)


def tower_kernel(
    near_ref, far_ref, first_ref, second_ref, unit_ref, scale_ref, bf_ref, slope_ref
):
    query_in = (near_ref[...] + far_ref[...].astype(jnp.float32)).astype(jnp.bfloat16)
    query_in = (0.5 * query_in.astype(jnp.float32)).astype(jnp.bfloat16)
    step = 1024
    total = None
    for at in range(0, first_ref.shape[1], step):
        pre = dot(query_in, first_ref[:, at : at + step])
        turn = jnp.tanh(pre)
        hidden = pre + pre * turn
        turn = 0.5 * turn
        slope_ref[:, at : at + step] = (0.5 + turn) + hidden * (0.5 - turn)
        part = dot(hidden.astype(jnp.bfloat16), second_ref[at : at + step, :])
        total = part if total is None else total + part
    unit, scale = unit_rows(total)
    unit_ref[...] = unit
    scale_ref[...] = scale
    bf_ref[...] = unit.astype(jnp.bfloat16)


def group_exps(query, item):
    return jnp.exp(INV_TEMP * row_dot(query, item))


def row_sums(values):
    return jnp.sum(values, axis=1, keepdims=True)


def query_grad_kernel(blocks, *refs):
    query_ref, items, refs = refs[0], refs[1 : 1 + blocks], refs[1 + blocks :]
    first_ref, second_ref, slope_ref, unit_ref, scale_ref, loss_ref, grad_ref, item_sum_ref = refs
    query = query_ref[...]
    kept = [group_exps(query, item[...]) for item in items[:2]]
    total = sum(row_sums(exps) for exps in kept)
    for item in items[2:]:
        total = total + row_sums(group_exps(query, item[...]))
    inverse = 1.0 / total
    query_sum = jnp.zeros(query.shape, jnp.float32)
    for j, item in enumerate(items):
        exps = kept[j] if j < 2 else group_exps(query, item[...])
        probs = (exps * inverse).astype(jnp.bfloat16)
        query_sum = query_sum + dot(probs, item[...])
        if j == 0:
            item_sum_ref[...] = col_dot(probs, query)
    wide_item = items[0][...].astype(jnp.float32)
    own = INV_TEMP * row_sums(query.astype(jnp.float32) * wide_item)
    loss_ref[...] = (jnp.log(total) - own).T
    out_grad = unit_backward(
        INV_TEMP * (query_sum - wide_item), unit_ref[...], scale_ref[...]
    ).astype(jnp.bfloat16)
    step = 1024
    total = None
    for at in range(0, first_ref.shape[1], step):
        back = row_dot(out_grad, second_ref[at : at + step, :])
        hidden_grad = (back * slope_ref[:, at : at + step]).astype(jnp.bfloat16)
        part = row_dot(hidden_grad, first_ref[:, at : at + step])
        total = part if total is None else total + part
    grad_ref[...] = total


def item_grad_kernel(blocks, *refs):
    queries, items, refs = refs[:blocks], refs[blocks : 2 * blocks], refs[2 * blocks :]
    item_sum_ref, unit_ref, scale_ref, loss_ref, query_grad_ref, grad_ref, *outs, sems = refs
    copies = [
        pltpu.make_async_copy(given, out, sems.at[i])
        for i, (given, out) in enumerate(zip((loss_ref, query_grad_ref), outs))
    ]
    for copy in copies:
        copy.start()
    item_sum = item_sum_ref[...]
    for i in range(1, blocks):
        query = queries[i][...]
        own_exps = group_exps(query, items[0][...])
        total = row_sums(own_exps)
        for j in range(1, blocks):
            total = total + row_sums(group_exps(query, items[j][...]))
        item_sum = item_sum + col_dot((own_exps * (1.0 / total)).astype(jnp.bfloat16), query)
    grad_ref[...] = unit_backward(
        INV_TEMP * (item_sum - queries[0][...].astype(jnp.float32)), unit_ref[...], scale_ref[...]
    )
    for copy in copies:
        copy.wait()


def rotated(shard, axis, by):
    count = lax.axis_size(axis)
    return lax.ppermute(shard, axis, [(i, (i + by) % count) for i in range(count)])


def struct(shape, dtype):
    return jax.ShapeDtypeStruct(shape, dtype)


def local(id_table, w_first, w_second, owner_ids, row_ids):
    pairs, bags = owner_ids.shape
    shards = lax.axis_size("table")
    blocks = lax.axis_size("blk")
    width = id_table.shape[1]
    hidden_units = w_first.shape[1]
    capacity = min(pairs, 3 * pairs * bags // (2 * shards))
    bf, f32 = jnp.bfloat16, jnp.float32

    half = shards // 2
    chips = half // 2
    power = chips & (chips - 1) == 0

    def relative(chip, j):
        return chip ^ j if power else (chip + j) % chips

    def to_chip(values, j, flip=0):
        if j == 0 and flip == 0:
            return values
        route = [
            (t, t // half * half + relative(t % half // 2, j) * 2 + (t % 2 ^ flip))
            for t in range(shards)
        ]
        return lax.ppermute(values, "table", route)

    def to_mirror(values):
        return lax.ppermute(values, "table", [(t, (t + half) % shards) for t in range(shards)])

    code = owner_ids * id_table.shape[0] + row_ids
    mirror_code = to_mirror(code)
    codes = [code, to_chip(code, 0, 1), mirror_code, to_chip(mirror_code, 0, 1)]
    touched = pl.pallas_call(
        touch_kernel,
        in_specs=[pl.BlockSpec(memory_space=pl.ANY)],
        out_shape=struct((16, width), f32),
        scratch_shapes=[pltpu.VMEM((16, width), bf), pltpu.SemaphoreType.DMA(())],
        compiler_params=params(52),
        name="touch",
    )(id_table)
    wide = pl.pallas_call(
        widen_kernel,
        out_shape=struct((2 * id_table.shape[0], width // 2), f32),
        compiler_params=params(8),
        name="widen",
    )(id_table)
    codes = [c.T for c in codes]
    requests = pl.pallas_call(
        functools.partial(route_kernel, relative, id_table.shape[0]),
        out_shape=[struct((4, capacity), jnp.int32)] * chips,
        compiler_params=params(4),
        name="route",
    )(*codes, touched)
    *codes, _ = lax.optimization_barrier((*codes, requests[0]))
    near_bags, far_bags = pl.pallas_call(
        functools.partial(bag_kernel, relative, id_table.shape[0]),
        out_shape=[struct((half, capacity), jnp.int32)] * 2,
        compiler_params=params(4),
        name="bag_lists",
    )(*codes)
    wanted = [to_chip(requests[j], j) for j in reversed(range(chips))][::-1]

    wide, near_bags, far_bags = lax.optimization_barrier((wide, near_bags, far_bags))

    def gather(askers):
        return pl.pallas_call(
            functools.partial(gather_kernel, chips, askers),
            in_specs=[pl.BlockSpec(memory_space=pl.ANY)] * chips
            + [pl.BlockSpec(memory_space=pltpu.VMEM)],
            out_shape=[struct((chips, capacity, width), bf)] * len(askers),
            scratch_shapes=[
                pltpu.SMEM((chips, 4, capacity), jnp.int32),
                pltpu.VMEM((2 * capacity, width // 2), f32),
                pltpu.SemaphoreType.DMA((chips,)),
            ],
            compiler_params=params(8),
            name="gather",
        )(*wanted[::-1], wide)

    order = list(range(chips - 1, 0, -1))

    def answered(same, swapped):
        messages = pl.pallas_call(
            functools.partial(pack_kernel, chips),
            out_shape=[struct((2, capacity, width), bf)] * (chips - 1),
            compiler_params=params(8),
            name="pack",
        )(same, swapped)
        arrived = []
        for j in order:
            back = j if power else (chips - j) % chips
            arrived.append(to_chip(messages[chips - 1 - back], back))
        return (same, swapped, *arrived), messages

    far_other, near_other = [to_chip(rows, 0, 1) for rows in gather((3, 1))]
    (far_same,), (near_same,) = gather((2,)), gather((0,))
    far_rows, _ = answered(far_same, far_other)
    near_rows, near_messages = answered(near_same, near_other)
    far_bags, _ = lax.optimization_barrier((far_bags, near_messages[-1]))

    def sums(kind, bags, rows, dtype):
        return pl.pallas_call(
            functools.partial(sum_kernel, order, kind),
            out_shape=struct((pairs, width), dtype),
            compiler_params=params(8),
            name="item_sums" if kind else "query_sums",
        )(bags, *rows)

    far_item = sums(1, far_bags, far_rows, bf)
    far_bags, _ = lax.optimization_barrier((far_bags, far_item))
    far_query = to_mirror(sums(0, far_bags, far_rows, bf))
    far_item = to_mirror(far_item)
    item_unit, item_scale, item_bf = pl.pallas_call(
        functools.partial(item_kernel, order),
        out_shape=[
            struct((pairs, width), f32),
            struct((pairs, 1), f32),
            struct((pairs, width), bf),
        ],
        compiler_params=params(8),
        name="items",
    )(near_bags, far_item, *near_rows)
    near_bags, _ = lax.optimization_barrier((near_bags, item_bf))
    near_query = sums(0, near_bags, near_rows, f32)
    items = [item_bf] + [rotated(item_bf, "blk", by) for by in range(1, blocks)]
    query_unit, query_scale, query_bf, slope = pl.pallas_call(
        tower_kernel,
        out_shape=[
            struct((pairs, width), f32),
            struct((pairs, 1), f32),
            struct((pairs, width), bf),
            struct((pairs, hidden_units), f32),
        ],
        compiler_params=params(12),
        name="tower",
    )(near_query, far_query, w_first, w_second)
    queries = [query_bf] + [rotated(query_bf, "blk", by) for by in range(1, blocks)]
    loss, query_grad, own_sum = pl.pallas_call(
        functools.partial(query_grad_kernel, blocks),
        out_shape=[
            struct((1, pairs), f32),
            struct((pairs, width), f32),
            struct((pairs, width), f32),
        ],
        compiler_params=params(12),
        name="query_grads",
    )(query_bf, *items, w_first, w_second, slope, query_unit, query_scale)
    queries, loss = lax.optimization_barrier((queries, loss))
    in_vmem, anywhere = pl.BlockSpec(memory_space=pltpu.VMEM), pl.BlockSpec(memory_space=pl.ANY)
    item_grad, loss, query_grad = pl.pallas_call(
        functools.partial(item_grad_kernel, blocks),
        in_specs=[in_vmem] * (2 * blocks + 3) + [anywhere] * 2,
        out_specs=[in_vmem, anywhere, anywhere],
        out_shape=[
            struct((pairs, width), f32),
            struct((1, pairs), f32),
            struct((pairs, width), f32),
        ],
        scratch_shapes=[pltpu.SemaphoreType.DMA((2,))],
        compiler_params=params(12),
        name="item_grads",
    )(*queries, *items, own_sum, item_unit, item_scale, loss, query_grad)
    return loss.reshape(pairs), item_grad, query_grad


def solution(mesh):
    placed = (P("table", None), P(), P(), P(("blk", "table"), None), P(("blk", "table"), None))
    return jax.shard_map(
        local,
        mesh=mesh,
        in_specs=placed,
        out_specs=(P(("blk", "table")), P(("blk", "table"), None), P(("blk", "table"), None)),
        check_vma=False,
    )
```

```python
import functools

import jax
import jax.numpy as jnp
from jax import lax
from jax.experimental import pallas as pl
from jax.experimental.pallas import tpu as pltpu
from jax.sharding import PartitionSpec as P

EPS = 1e-06
INV_TEMP = 20.0


def params(mebibytes):
    return pltpu.CompilerParams(vmem_limit_bytes=mebibytes * 1024 * 1024)


def iota(shape, dim):
    return lax.broadcasted_iota(jnp.int32, shape, dim)


def row_dot(left, right):
    return lax.dot_general(
        left, right, (((1,), (1,)), ((), ())), preferred_element_type=jnp.float32
    )


def col_dot(left, right):
    return lax.dot_general(
        left, right, (((0,), (0,)), ((), ())), preferred_element_type=jnp.float32
    )


def dot(left, right):
    return jnp.dot(left, right, preferred_element_type=jnp.float32)


def unit_rows(vectors):
    scale = lax.rsqrt(jnp.sum(vectors * vectors, axis=-1, keepdims=True) + EPS)
    return vectors * scale, scale


def unit_backward(grad, unit, scale):
    return scale * (grad - unit * jnp.sum(unit * grad, axis=-1, keepdims=True))


def packed_lists(relative, rows_dev, askers, codes, chips, capacity):
    bags, pairs = codes[0].shape
    lists = len(askers) * chips
    place = lax.axis_index("table")
    half = 2 * chips
    list_of = iota((lists, pairs), 0)
    chip = relative(place % half // 2, list_of % chips)
    asker = list_of // chips
    core = place % 2
    for at, name in enumerate(askers):
        if name >= 4:
            core = jnp.where(asker == at, 1 - place % 2, core)
    start = (place // half * half + chip * 2 + core) * rows_dev
    named = jnp.zeros((lists, pairs), jnp.float32)
    rows = jnp.zeros((lists, pairs), jnp.int32)
    kind = jnp.zeros((lists, pairs), jnp.int32)
    for k in range(bags):
        code = codes[(0, 1, 2, 3, 0, 2)[askers[0]]][k : k + 1, :]
        for at, name in enumerate(askers[1:], 1):
            code = jnp.where(asker == at, codes[(0, 1, 2, 3, 0, 2)[name]][k : k + 1, :], code)
        row = code - start
        hit = (row >= 0) & (row < rows_dev)
        named = jnp.where(hit, 1.0, named)
        rows = jnp.where(hit, row, rows)
        kind = jnp.where(hit, 1 if k < bags // 2 else 2, kind)
    before = jnp.where(iota((pairs, pairs), 0) < iota((pairs, pairs), 1), 1.0, 0.0)
    slot = dot(named.astype(jnp.bfloat16), before.astype(jnp.bfloat16)).astype(jnp.int32)
    slot = jnp.where(named > 0.0, slot, -1)
    digits = [rows // 256, rows % 256, kind, iota((lists, pairs), 1)]
    packed = jnp.concatenate([d.astype(jnp.float32) for d in digits], axis=0).astype(jnp.bfloat16)
    places = iota((capacity, pairs), 0)
    for s in range(lists):
        chosen = jnp.where(slot[s : s + 1, :] == places, 1.0, 0.0).astype(jnp.bfloat16)
        got = row_dot(packed, chosen).astype(jnp.int32)
        high, low, which, pair = [got[i * lists + s : i * lists + s + 1, :] for i in range(4)]
        yield s // chips, s % chips, high * 256 + low, which, pair


def route_kernel(relative, rows_dev, *refs):
    codes, requests = refs[:4], refs[5:]
    capacity = requests[0].shape[1]
    lists = packed_lists(relative, rows_dev, (0, 1, 2, 3), codes, len(requests), capacity)
    for at, j, row, _, _ in lists:
        requests[j][at : at + 1, :] = 2 * row


def bag_kernel(relative, rows_dev, *refs):
    codes, outs = refs[:4], refs[4:]
    half, capacity = outs[0].shape
    pairs = codes[0].shape[1]
    chips = half // 2
    lists = packed_lists(relative, rows_dev, (0, 4, 2, 5), codes, chips, capacity)
    for at, j, _, which, pair in lists:
        place = at % 2 * chips + j
        outs[at // 2][place : place + 1, :] = (which - 1) * pairs + pair


def touch_kernel(table_hbm, out_ref, rows_ref, sem):
    copy = pltpu.make_async_copy(table_hbm.at[pl.ds(0, rows_ref.shape[0]), :], rows_ref, sem)
    copy.start()
    copy.wait()
    out_ref[...] = rows_ref[...].astype(jnp.float32)


def widen_kernel(table_ref, wide_ref):
    width = table_ref.shape[1]
    step = 128

    def widen(i, carry):
        start = pl.multiple_of(i * step, step)
        part = table_ref[pl.ds(start, step), :].astype(jnp.float32)
        wide_ref[pl.ds(2 * start, step, stride=2), :] = part[:, : width // 2]
        wide_ref[pl.ds(2 * start + 1, step, stride=2), :] = part[:, width // 2 :]
        return carry

    lax.fori_loop(0, table_ref.shape[0] // step, widen, 0)


def gather_kernel(chips, askers, *refs):
    wanted, wide_ref, refs = refs[:chips], refs[chips], refs[chips + 1 :]
    outs, (index_ref, stage, sems) = refs[: len(askers)], refs[len(askers) :]
    _, capacity, width = outs[0].shape
    group = 16
    copies = [
        pltpu.make_async_copy(wanted[chips - 1 - j], index_ref.at[j], sems.at[j])
        for j in range(chips)
    ]
    for copy in copies:
        copy.start()
    for copy in copies:
        copy.wait()
    for asker, out_ref in zip(askers, outs):
        for j in range(chips):
            for base in range(0, capacity, group):
                found = [
                    wide_ref[pl.ds(index_ref[j, asker, base + i], 2), :] for i in range(group)
                ]
                for i in range(group):
                    stage[pl.ds(2 * (base + i), 2), :] = found[i]
            for part in range(2):
                values = stage[pl.ds(part, capacity, stride=2), :]
                out_ref[j, :, part * (width // 2) : (part + 1) * (width // 2)] = values.astype(
                    jnp.bfloat16
                )


def pack_kernel(chips, same_ref, swapped_ref, *out_refs):
    for out_ref, j in zip(out_refs, range(chips - 1, 0, -1)):
        out_ref[0] = same_ref[j]
        out_ref[1] = swapped_ref[j]


def bag_sums(bag_ref, rows, bags, first):
    total = None
    for at, values in enumerate(rows):
        chosen = bag_ref[at : at + 1, :] == first + iota((bags, bag_ref.shape[1]), 0)
        part = dot(jnp.where(chosen, 1.0, 0.0).astype(jnp.bfloat16), values)
        total = part if total is None else total + part
    return total


def lists_of(order, same_ref, swapped_ref, message_refs):
    chips = len(order) + 1
    return [
        own_ref[0] if j == 0 else message_refs[order.index(j)][f]
        for f, own_ref in enumerate((same_ref, swapped_ref))
        for j in range(chips)
    ]


def sum_kernel(order, kind, bag_ref, same_ref, swapped_ref, *refs):
    out_ref = refs[-1]
    pairs = out_ref.shape[0]
    rows = lists_of(order, same_ref, swapped_ref, refs[:-1])
    out_ref[...] = bag_sums(bag_ref, rows, pairs, kind * pairs).astype(out_ref.dtype)


def item_kernel(order, bag_ref, far_ref, same_ref, swapped_ref, *refs):
    messages, (unit_ref, scale_ref, bf_ref) = refs[:-3], refs[-3:]
    pairs = bf_ref.shape[0]
    rows = lists_of(order, same_ref, swapped_ref, messages)
    total = bag_sums(bag_ref, rows, pairs, pairs) + far_ref[...].astype(jnp.float32)
    unit, scale = unit_rows(total)
    unit_ref[...] = unit
    scale_ref[...] = scale
    bf_ref[...] = unit.astype(jnp.bfloat16)


def tower_kernel(
    near_ref, far_ref, first_ref, second_ref, unit_ref, scale_ref, bf_ref, slope_ref
):
    query_in = (near_ref[...] + far_ref[...].astype(jnp.float32)).astype(jnp.bfloat16)
    query_in = (0.5 * query_in.astype(jnp.float32)).astype(jnp.bfloat16)
    step = 1024
    total = None
    for at in range(0, first_ref.shape[1], step):
        pre = dot(query_in, first_ref[:, at : at + step])
        turn = jnp.tanh(pre)
        hidden = pre + pre * turn
        turn = 0.5 * turn
        slope_ref[:, at : at + step] = (0.5 + turn) + hidden * (0.5 - turn)
        part = dot(hidden.astype(jnp.bfloat16), second_ref[at : at + step, :])
        total = part if total is None else total + part
    unit, scale = unit_rows(total)
    unit_ref[...] = unit
    scale_ref[...] = scale
    bf_ref[...] = unit.astype(jnp.bfloat16)


def group_exps(query, item):
    return jnp.exp(INV_TEMP * row_dot(query, item))


def row_sums(values):
    return jnp.sum(values, axis=1, keepdims=True)


def query_grad_kernel(blocks, *refs):
    query_ref, items, refs = refs[0], refs[1 : 1 + blocks], refs[1 + blocks :]
    first_ref, second_ref, slope_ref, unit_ref, scale_ref, loss_ref, grad_ref, item_sum_ref = refs
    query = query_ref[...]
    kept = [group_exps(query, item[...]) for item in items[:2]]
    total = sum(row_sums(exps) for exps in kept)
    for item in items[2:]:
        total = total + row_sums(group_exps(query, item[...]))
    inverse = 1.0 / total
    query_sum = jnp.zeros(query.shape, jnp.float32)
    for j, item in enumerate(items):
        exps = kept[j] if j < 2 else group_exps(query, item[...])
        probs = (exps * inverse).astype(jnp.bfloat16)
        query_sum = query_sum + dot(probs, item[...])
        if j == 0:
            item_sum_ref[...] = col_dot(probs, query)
    wide_item = items[0][...].astype(jnp.float32)
    own = INV_TEMP * row_sums(query.astype(jnp.float32) * wide_item)
    loss_ref[...] = (jnp.log(total) - own).T
    out_grad = unit_backward(
        INV_TEMP * (query_sum - wide_item), unit_ref[...], scale_ref[...]
    ).astype(jnp.bfloat16)
    step = 1024
    total = None
    for at in range(0, first_ref.shape[1], step):
        back = row_dot(out_grad, second_ref[at : at + step, :])
        hidden_grad = (back * slope_ref[:, at : at + step]).astype(jnp.bfloat16)
        part = row_dot(hidden_grad, first_ref[:, at : at + step])
        total = part if total is None else total + part
    grad_ref[...] = total


def item_grad_kernel(blocks, *refs):
    queries, items, refs = refs[:blocks], refs[blocks : 2 * blocks], refs[2 * blocks :]
    item_sum_ref, unit_ref, scale_ref, loss_ref, query_grad_ref, grad_ref, *outs, sems = refs
    copies = [
        pltpu.make_async_copy(given, out, sems.at[i])
        for i, (given, out) in enumerate(zip((loss_ref, query_grad_ref), outs))
    ]
    for copy in copies:
        copy.start()
    item_sum = item_sum_ref[...]
    for i in range(1, blocks):
        query = queries[i][...]
        own_exps = group_exps(query, items[0][...])
        total = row_sums(own_exps)
        for j in range(1, blocks):
            total = total + row_sums(group_exps(query, items[j][...]))
        item_sum = item_sum + col_dot((own_exps * (1.0 / total)).astype(jnp.bfloat16), query)
    grad_ref[...] = unit_backward(
        INV_TEMP * (item_sum - queries[0][...].astype(jnp.float32)), unit_ref[...], scale_ref[...]
    )
    for copy in copies:
        copy.wait()


def rotated(shard, axis, by):
    count = lax.axis_size(axis)
    return lax.ppermute(shard, axis, [(i, (i + by) % count) for i in range(count)])


def struct(shape, dtype):
    return jax.ShapeDtypeStruct(shape, dtype)


def local(id_table, w_first, w_second, owner_ids, row_ids):
    pairs, bags = owner_ids.shape
    shards = lax.axis_size("table")
    blocks = lax.axis_size("blk")
    width = id_table.shape[1]
    hidden_units = w_first.shape[1]
    capacity = min(pairs, 3 * pairs * bags // (2 * shards))
    bf, f32 = jnp.bfloat16, jnp.float32

    half = shards // 2
    chips = half // 2
    power = chips & (chips - 1) == 0

    def relative(chip, j):
        return chip ^ j if power else (chip + j) % chips

    def to_chip(values, j, flip=0):
        if j == 0 and flip == 0:
            return values
        route = [
            (t, t // half * half + relative(t % half // 2, j) * 2 + (t % 2 ^ flip))
            for t in range(shards)
        ]
        return lax.ppermute(values, "table", route)

    def to_mirror(values):
        return lax.ppermute(values, "table", [(t, (t + half) % shards) for t in range(shards)])

    code = owner_ids * id_table.shape[0] + row_ids
    mirror_code = to_mirror(code)
    codes = [code, to_chip(code, 0, 1), mirror_code, to_chip(mirror_code, 0, 1)]
    touched = pl.pallas_call(
        touch_kernel,
        in_specs=[pl.BlockSpec(memory_space=pl.ANY)],
        out_shape=struct((16, width), f32),
        scratch_shapes=[pltpu.VMEM((16, width), bf), pltpu.SemaphoreType.DMA(())],
        compiler_params=params(52),
        name="touch",
    )(id_table)
    wide = pl.pallas_call(
        widen_kernel,
        out_shape=struct((2 * id_table.shape[0], width // 2), f32),
        compiler_params=params(8),
        name="widen",
    )(id_table)
    codes = [c.T for c in codes]
    requests = pl.pallas_call(
        functools.partial(route_kernel, relative, id_table.shape[0]),
        out_shape=[struct((4, capacity), jnp.int32)] * chips,
        compiler_params=params(4),
        name="route",
    )(*codes, touched)
    *codes, _ = lax.optimization_barrier((*codes, requests[0]))
    near_bags, far_bags = pl.pallas_call(
        functools.partial(bag_kernel, relative, id_table.shape[0]),
        out_shape=[struct((half, capacity), jnp.int32)] * 2,
        compiler_params=params(4),
        name="bag_lists",
    )(*codes)
    wanted = [to_chip(requests[j], j) for j in reversed(range(chips))][::-1]

    wide, near_bags, far_bags = lax.optimization_barrier((wide, near_bags, far_bags))

    def gather(askers):
        return pl.pallas_call(
            functools.partial(gather_kernel, chips, askers),
            in_specs=[pl.BlockSpec(memory_space=pl.ANY)] * chips
            + [pl.BlockSpec(memory_space=pltpu.VMEM)],
            out_shape=[struct((chips, capacity, width), bf)] * len(askers),
            scratch_shapes=[
                pltpu.SMEM((chips, 4, capacity), jnp.int32),
                pltpu.VMEM((2 * capacity, width // 2), f32),
                pltpu.SemaphoreType.DMA((chips,)),
            ],
            compiler_params=params(8),
            name="gather",
        )(*wanted[::-1], wide)

    order = list(range(1, chips))

    def answered(same, swapped):
        messages = pl.pallas_call(
            functools.partial(pack_kernel, chips),
            out_shape=[struct((2, capacity, width), bf)] * (chips - 1),
            compiler_params=params(8),
            name="pack",
        )(same, swapped)
        arrived = []
        for j in order:
            back = j if power else (chips - j) % chips
            arrived.append(to_chip(messages[chips - 1 - back], back))
        return (same, swapped, *arrived), messages

    far_other, near_other = [to_chip(rows, 0, 1) for rows in gather((3, 1))]
    (far_same,), (near_same,) = gather((2,)), gather((0,))
    far_rows, _ = answered(far_same, far_other)
    near_rows, near_messages = answered(near_same, near_other)
    far_bags, _ = lax.optimization_barrier((far_bags, near_messages[0]))

    def sums(kind, bags, rows, dtype):
        return pl.pallas_call(
            functools.partial(sum_kernel, order, kind),
            out_shape=struct((pairs, width), dtype),
            compiler_params=params(8),
            name="item_sums" if kind else "query_sums",
        )(bags, *rows)

    far_item = sums(1, far_bags, far_rows, bf)
    far_bags, _ = lax.optimization_barrier((far_bags, far_item))
    far_query = to_mirror(sums(0, far_bags, far_rows, bf))
    far_item = to_mirror(far_item)
    item_unit, item_scale, item_bf = pl.pallas_call(
        functools.partial(item_kernel, order),
        out_shape=[
            struct((pairs, width), f32),
            struct((pairs, 1), f32),
            struct((pairs, width), bf),
        ],
        compiler_params=params(8),
        name="items",
    )(near_bags, far_item, *near_rows)
    near_bags, _ = lax.optimization_barrier((near_bags, item_bf))
    near_query = sums(0, near_bags, near_rows, f32)
    items = [item_bf] + [rotated(item_bf, "blk", by) for by in range(1, blocks)]
    query_unit, query_scale, query_bf, slope = pl.pallas_call(
        tower_kernel,
        out_shape=[
            struct((pairs, width), f32),
            struct((pairs, 1), f32),
            struct((pairs, width), bf),
            struct((pairs, hidden_units), f32),
        ],
        compiler_params=params(12),
        name="tower",
    )(near_query, far_query, w_first, w_second)
    queries = [query_bf] + [rotated(query_bf, "blk", by) for by in range(1, blocks)]
    loss, query_grad, own_sum = pl.pallas_call(
        functools.partial(query_grad_kernel, blocks),
        out_shape=[
            struct((1, pairs), f32),
            struct((pairs, width), f32),
            struct((pairs, width), f32),
        ],
        compiler_params=params(12),
        name="query_grads",
    )(query_bf, *items, w_first, w_second, slope, query_unit, query_scale)
    queries, loss = lax.optimization_barrier((queries, loss))
    in_vmem, anywhere = pl.BlockSpec(memory_space=pltpu.VMEM), pl.BlockSpec(memory_space=pl.ANY)
    item_grad, loss, query_grad = pl.pallas_call(
        functools.partial(item_grad_kernel, blocks),
        in_specs=[in_vmem] * (2 * blocks + 3) + [anywhere] * 2,
        out_specs=[in_vmem, anywhere, anywhere],
        out_shape=[
            struct((pairs, width), f32),
            struct((1, pairs), f32),
            struct((pairs, width), f32),
        ],
        scratch_shapes=[pltpu.SemaphoreType.DMA((2,))],
        compiler_params=params(12),
        name="item_grads",
    )(*queries, *items, own_sum, item_unit, item_scale, loss, query_grad)
    return loss.reshape(pairs), item_grad, query_grad


def solution(mesh):
    placed = (P("table", None), P(), P(), P(("blk", "table"), None), P(("blk", "table"), None))
    return jax.shard_map(
        local,
        mesh=mesh,
        in_specs=placed,
        out_specs=(P(("blk", "table")), P(("blk", "table"), None), P(("blk", "table"), None)),
        check_vma=False,
    )
```

```python
import functools

import jax
import jax.numpy as jnp
from jax import lax
from jax.experimental import pallas as pl
from jax.experimental.pallas import tpu as pltpu
from jax.sharding import PartitionSpec as P

EPS = 1e-06
INV_TEMP = 20.0


def params(mebibytes):
    return pltpu.CompilerParams(vmem_limit_bytes=mebibytes * 1024 * 1024)


def iota(shape, dim):
    return lax.broadcasted_iota(jnp.int32, shape, dim)


def row_dot(left, right):
    return lax.dot_general(
        left, right, (((1,), (1,)), ((), ())), preferred_element_type=jnp.float32
    )


def col_dot(left, right):
    return lax.dot_general(
        left, right, (((0,), (0,)), ((), ())), preferred_element_type=jnp.float32
    )


def dot(left, right):
    return jnp.dot(left, right, preferred_element_type=jnp.float32)


def unit_rows(vectors):
    scale = lax.rsqrt(jnp.sum(vectors * vectors, axis=-1, keepdims=True) + EPS)
    return vectors * scale, scale


def unit_backward(grad, unit, scale):
    return scale * (grad - unit * jnp.sum(unit * grad, axis=-1, keepdims=True))


def packed_lists(relative, rows_dev, askers, codes, chips, capacity):
    bags, pairs = codes[0].shape
    lists = len(askers) * chips
    place = lax.axis_index("table")
    half = 2 * chips
    list_of = iota((lists, pairs), 0)
    chip = relative(place % half // 2, list_of % chips)
    asker = list_of // chips
    core = place % 2
    for at, name in enumerate(askers):
        if name >= 4:
            core = jnp.where(asker == at, 1 - place % 2, core)
    start = (place // half * half + chip * 2 + core) * rows_dev
    named = jnp.zeros((lists, pairs), jnp.float32)
    rows = jnp.zeros((lists, pairs), jnp.int32)
    kind = jnp.zeros((lists, pairs), jnp.int32)
    for k in range(bags):
        code = codes[(0, 1, 2, 3, 0, 2)[askers[0]]][k : k + 1, :]
        for at, name in enumerate(askers[1:], 1):
            code = jnp.where(asker == at, codes[(0, 1, 2, 3, 0, 2)[name]][k : k + 1, :], code)
        row = code - start
        hit = (row >= 0) & (row < rows_dev)
        named = jnp.where(hit, 1.0, named)
        rows = jnp.where(hit, row, rows)
        kind = jnp.where(hit, 1 if k < bags // 2 else 2, kind)
    before = jnp.where(iota((pairs, pairs), 0) < iota((pairs, pairs), 1), 1.0, 0.0)
    slot = dot(named.astype(jnp.bfloat16), before.astype(jnp.bfloat16)).astype(jnp.int32)
    slot = jnp.where(named > 0.0, slot, -1)
    digits = [rows // 256, rows % 256, kind, iota((lists, pairs), 1)]
    packed = jnp.concatenate([d.astype(jnp.float32) for d in digits], axis=0).astype(jnp.bfloat16)
    places = iota((capacity, pairs), 0)
    for s in range(lists):
        chosen = jnp.where(slot[s : s + 1, :] == places, 1.0, 0.0).astype(jnp.bfloat16)
        got = row_dot(packed, chosen).astype(jnp.int32)
        high, low, which, pair = [got[i * lists + s : i * lists + s + 1, :] for i in range(4)]
        yield s // chips, s % chips, high * 256 + low, which, pair


def route_kernel(relative, rows_dev, *refs):
    codes, requests = refs[:4], refs[5:]
    capacity = requests[0].shape[1]
    lists = packed_lists(relative, rows_dev, (0, 1, 2, 3), codes, len(requests), capacity)
    for at, j, row, _, _ in lists:
        requests[j][at : at + 1, :] = 2 * row


def bag_kernel(relative, rows_dev, *refs):
    codes, outs = refs[:4], refs[4:]
    half, capacity = outs[0].shape
    pairs = codes[0].shape[1]
    chips = half // 2
    lists = packed_lists(relative, rows_dev, (0, 4, 2, 5), codes, chips, capacity)
    for at, j, _, which, pair in lists:
        place = at % 2 * chips + j
        outs[at // 2][place : place + 1, :] = (which - 1) * pairs + pair


def touch_kernel(table_hbm, out_ref, rows_ref, sem):
    copy = pltpu.make_async_copy(table_hbm.at[pl.ds(0, rows_ref.shape[0]), :], rows_ref, sem)
    copy.start()
    copy.wait()
    out_ref[...] = rows_ref[...].astype(jnp.float32)


def widen_kernel(table_ref, wide_ref):
    width = table_ref.shape[1]
    step = 128

    def widen(i, carry):
        start = pl.multiple_of(i * step, step)
        part = table_ref[pl.ds(start, step), :].astype(jnp.float32)
        wide_ref[pl.ds(2 * start, step, stride=2), :] = part[:, : width // 2]
        wide_ref[pl.ds(2 * start + 1, step, stride=2), :] = part[:, width // 2 :]
        return carry

    lax.fori_loop(0, table_ref.shape[0] // step, widen, 0)


def gather_kernel(chips, askers, *refs):
    wanted, wide_ref, refs = refs[:chips], refs[chips], refs[chips + 1 :]
    outs, (index_ref, stage, sems) = refs[: len(askers)], refs[len(askers) :]
    _, capacity, width = outs[0].shape
    group = 16
    copies = [
        pltpu.make_async_copy(wanted[chips - 1 - j], index_ref.at[j], sems.at[j])
        for j in range(chips)
    ]
    for copy in copies:
        copy.start()
    for copy in copies:
        copy.wait()
    for asker, out_ref in zip(askers, outs):
        for j in range(chips):
            for base in range(0, capacity, group):
                found = [
                    wide_ref[pl.ds(index_ref[j, asker, base + i], 2), :] for i in range(group)
                ]
                for i in range(group):
                    stage[pl.ds(2 * (base + i), 2), :] = found[i]
            for part in range(2):
                values = stage[pl.ds(part, capacity, stride=2), :]
                out_ref[j, :, part * (width // 2) : (part + 1) * (width // 2)] = values.astype(
                    jnp.bfloat16
                )


def pack_kernel(chips, same_ref, swapped_ref, *out_refs):
    for out_ref, j in zip(out_refs, range(chips - 1, 0, -1)):
        out_ref[0] = same_ref[j]
        out_ref[1] = swapped_ref[j]


def bag_sums(bag_ref, rows, bags, first):
    total = None
    for at, values in enumerate(rows):
        chosen = bag_ref[at : at + 1, :] == first + iota((bags, bag_ref.shape[1]), 0)
        part = dot(jnp.where(chosen, 1.0, 0.0).astype(jnp.bfloat16), values)
        total = part if total is None else total + part
    return total


def lists_of(order, same_ref, swapped_ref, message_refs):
    chips = len(order) + 1
    return [
        own_ref[0] if j == 0 else message_refs[order.index(j)][f]
        for f, own_ref in enumerate((same_ref, swapped_ref))
        for j in range(chips)
    ]


def sum_kernel(order, kind, bag_ref, same_ref, swapped_ref, *refs):
    out_ref = refs[-1]
    pairs = out_ref.shape[0]
    rows = lists_of(order, same_ref, swapped_ref, refs[:-1])
    out_ref[...] = bag_sums(bag_ref, rows, pairs, kind * pairs).astype(out_ref.dtype)


def item_kernel(order, bag_ref, far_ref, same_ref, swapped_ref, *refs):
    messages, (unit_ref, scale_ref, bf_ref) = refs[:-3], refs[-3:]
    pairs = bf_ref.shape[0]
    rows = lists_of(order, same_ref, swapped_ref, messages)
    total = bag_sums(bag_ref, rows, pairs, pairs) + far_ref[...].astype(jnp.float32)
    unit, scale = unit_rows(total)
    unit_ref[...] = unit
    scale_ref[...] = scale
    bf_ref[...] = unit.astype(jnp.bfloat16)


def tower_kernel(
    near_ref, far_ref, first_ref, second_ref, unit_ref, scale_ref, bf_ref, slope_ref
):
    query_in = (near_ref[...] + far_ref[...].astype(jnp.float32)).astype(jnp.bfloat16)
    query_in = (0.5 * query_in.astype(jnp.float32)).astype(jnp.bfloat16)
    step = 1024
    total = None
    for at in range(0, first_ref.shape[1], step):
        pre = dot(query_in, first_ref[:, at : at + step])
        turn = jnp.tanh(pre)
        hidden = pre + pre * turn
        turn = 0.5 * turn
        slope_ref[:, at : at + step] = (0.5 + turn) + hidden * (0.5 - turn)
        part = dot(hidden.astype(jnp.bfloat16), second_ref[at : at + step, :])
        total = part if total is None else total + part
    unit, scale = unit_rows(total)
    unit_ref[...] = unit
    scale_ref[...] = scale
    bf_ref[...] = unit.astype(jnp.bfloat16)


def group_exps(query, item):
    return jnp.exp(INV_TEMP * row_dot(query, item))


def row_sums(values):
    return jnp.sum(values, axis=1, keepdims=True)


def query_grad_kernel(blocks, *refs):
    query_ref, items, refs = refs[0], refs[1 : 1 + blocks], refs[1 + blocks :]
    first_ref, second_ref, slope_ref, unit_ref, scale_ref, loss_ref, grad_ref, item_sum_ref = refs
    query = query_ref[...]
    kept = [group_exps(query, item[...]) for item in items[:2]]
    total = sum(row_sums(exps) for exps in kept)
    for item in items[2:]:
        total = total + row_sums(group_exps(query, item[...]))
    inverse = 1.0 / total
    query_sum = jnp.zeros(query.shape, jnp.float32)
    for j, item in enumerate(items):
        exps = kept[j] if j < 2 else group_exps(query, item[...])
        probs = (exps * inverse).astype(jnp.bfloat16)
        query_sum = query_sum + dot(probs, item[...])
        if j == 0:
            item_sum_ref[...] = col_dot(probs, query)
    wide_item = items[0][...].astype(jnp.float32)
    own = INV_TEMP * row_sums(query.astype(jnp.float32) * wide_item)
    loss_ref[...] = (jnp.log(total) - own).T
    out_grad = unit_backward(
        INV_TEMP * (query_sum - wide_item), unit_ref[...], scale_ref[...]
    ).astype(jnp.bfloat16)
    step = 1024
    total = None
    for at in range(0, first_ref.shape[1], step):
        back = row_dot(out_grad, second_ref[at : at + step, :])
        hidden_grad = (back * slope_ref[:, at : at + step]).astype(jnp.bfloat16)
        part = row_dot(hidden_grad, first_ref[:, at : at + step])
        total = part if total is None else total + part
    grad_ref[...] = total


def item_grad_kernel(blocks, *refs):
    queries, items, refs = refs[:blocks], refs[blocks : 2 * blocks], refs[2 * blocks :]
    item_sum_ref, unit_ref, scale_ref, loss_ref, query_grad_ref, grad_ref, *outs, sems = refs
    copies = [
        pltpu.make_async_copy(given, out, sems.at[i])
        for i, (given, out) in enumerate(zip((loss_ref, query_grad_ref), outs))
    ]
    for copy in copies:
        copy.start()
    item_sum = item_sum_ref[...]
    for i in range(1, blocks):
        query = queries[i][...]
        own_exps = group_exps(query, items[0][...])
        total = row_sums(own_exps)
        for j in range(1, blocks):
            total = total + row_sums(group_exps(query, items[j][...]))
        item_sum = item_sum + col_dot((own_exps * (1.0 / total)).astype(jnp.bfloat16), query)
    grad_ref[...] = unit_backward(
        INV_TEMP * (item_sum - queries[0][...].astype(jnp.float32)), unit_ref[...], scale_ref[...]
    )
    for copy in copies:
        copy.wait()


def rotated(shard, axis, by):
    count = lax.axis_size(axis)
    return lax.ppermute(shard, axis, [(i, (i + by) % count) for i in range(count)])


def struct(shape, dtype):
    return jax.ShapeDtypeStruct(shape, dtype)


def local(id_table, w_first, w_second, owner_ids, row_ids):
    pairs, bags = owner_ids.shape
    shards = lax.axis_size("table")
    blocks = lax.axis_size("blk")
    width = id_table.shape[1]
    hidden_units = w_first.shape[1]
    capacity = min(pairs, 3 * pairs * bags // (2 * shards))
    bf, f32 = jnp.bfloat16, jnp.float32

    half = shards // 2
    chips = half // 2
    power = chips & (chips - 1) == 0

    def relative(chip, j):
        return chip ^ j if power else (chip + j) % chips

    def to_chip(values, j, flip=0):
        if j == 0 and flip == 0:
            return values
        route = [
            (t, t // half * half + relative(t % half // 2, j) * 2 + (t % 2 ^ flip))
            for t in range(shards)
        ]
        return lax.ppermute(values, "table", route)

    def to_mirror(values):
        return lax.ppermute(values, "table", [(t, (t + half) % shards) for t in range(shards)])

    code = owner_ids * id_table.shape[0] + row_ids
    mirror_code = to_mirror(code)
    codes = [code, to_chip(code, 0, 1), mirror_code, to_chip(mirror_code, 0, 1)]
    touched = pl.pallas_call(
        touch_kernel,
        in_specs=[pl.BlockSpec(memory_space=pl.ANY)],
        out_shape=struct((16, width), f32),
        scratch_shapes=[pltpu.VMEM((16, width), bf), pltpu.SemaphoreType.DMA(())],
        compiler_params=params(52),
        name="touch",
    )(id_table)
    wide = pl.pallas_call(
        widen_kernel,
        out_shape=struct((2 * id_table.shape[0], width // 2), f32),
        compiler_params=params(8),
        name="widen",
    )(id_table)
    codes = [c.T for c in codes]
    requests = pl.pallas_call(
        functools.partial(route_kernel, relative, id_table.shape[0]),
        out_shape=[struct((4, capacity), jnp.int32)] * chips,
        compiler_params=params(4),
        name="route",
    )(*codes, touched)
    *codes, _ = lax.optimization_barrier((*codes, requests[0]))
    near_bags, far_bags = pl.pallas_call(
        functools.partial(bag_kernel, relative, id_table.shape[0]),
        out_shape=[struct((half, capacity), jnp.int32)] * 2,
        compiler_params=params(4),
        name="bag_lists",
    )(*codes)
    wanted = [to_chip(requests[j], j) for j in reversed(range(chips))][::-1]

    wide, near_bags, far_bags = lax.optimization_barrier((wide, near_bags, far_bags))

    def gather(askers):
        return pl.pallas_call(
            functools.partial(gather_kernel, chips, askers),
            in_specs=[pl.BlockSpec(memory_space=pl.ANY)] * chips
            + [pl.BlockSpec(memory_space=pltpu.VMEM)],
            out_shape=[struct((chips, capacity, width), bf)] * len(askers),
            scratch_shapes=[
                pltpu.SMEM((chips, 4, capacity), jnp.int32),
                pltpu.VMEM((2 * capacity, width // 2), f32),
                pltpu.SemaphoreType.DMA((chips,)),
            ],
            compiler_params=params(8),
            name="gather",
        )(*wanted[::-1], wide)

    order = list(range(1, chips))

    def answered(same, swapped):
        messages = pl.pallas_call(
            functools.partial(pack_kernel, chips),
            out_shape=[struct((2, capacity, width), bf)] * (chips - 1),
            compiler_params=params(8),
            name="pack",
        )(same, swapped)
        arrived = []
        for j in order:
            back = j if power else (chips - j) % chips
            arrived.append(to_chip(messages[chips - 1 - back], back))
        return (same, swapped, *arrived), messages

    far_other, near_other = [to_chip(rows, 0, 1) for rows in gather((3, 1))]
    (far_same,), (near_same,) = gather((2,)), gather((0,))
    far_rows, _ = answered(far_same, far_other)
    near_same, near_other, _ = lax.optimization_barrier((near_same, near_other, far_rows[2]))
    near_rows, near_messages = answered(near_same, near_other)
    far_bags, _ = lax.optimization_barrier((far_bags, near_messages[0]))

    def sums(kind, bags, rows, dtype):
        return pl.pallas_call(
            functools.partial(sum_kernel, order, kind),
            out_shape=struct((pairs, width), dtype),
            compiler_params=params(8),
            name="item_sums" if kind else "query_sums",
        )(bags, *rows)

    far_item = sums(1, far_bags, far_rows, bf)
    far_bags, _ = lax.optimization_barrier((far_bags, far_item))
    far_query = to_mirror(sums(0, far_bags, far_rows, bf))
    far_item = to_mirror(far_item)
    item_unit, item_scale, item_bf = pl.pallas_call(
        functools.partial(item_kernel, order),
        out_shape=[
            struct((pairs, width), f32),
            struct((pairs, 1), f32),
            struct((pairs, width), bf),
        ],
        compiler_params=params(8),
        name="items",
    )(near_bags, far_item, *near_rows)
    near_bags, _ = lax.optimization_barrier((near_bags, item_bf))
    near_query = sums(0, near_bags, near_rows, f32)
    items = [item_bf] + [rotated(item_bf, "blk", by) for by in range(1, blocks)]
    query_unit, query_scale, query_bf, slope = pl.pallas_call(
        tower_kernel,
        out_shape=[
            struct((pairs, width), f32),
            struct((pairs, 1), f32),
            struct((pairs, width), bf),
            struct((pairs, hidden_units), f32),
        ],
        compiler_params=params(12),
        name="tower",
    )(near_query, far_query, w_first, w_second)
    queries = [query_bf] + [rotated(query_bf, "blk", by) for by in range(1, blocks)]
    loss, query_grad, own_sum = pl.pallas_call(
        functools.partial(query_grad_kernel, blocks),
        out_shape=[
            struct((1, pairs), f32),
            struct((pairs, width), f32),
            struct((pairs, width), f32),
        ],
        compiler_params=params(12),
        name="query_grads",
    )(query_bf, *items, w_first, w_second, slope, query_unit, query_scale)
    queries, loss = lax.optimization_barrier((queries, loss))
    in_vmem, anywhere = pl.BlockSpec(memory_space=pltpu.VMEM), pl.BlockSpec(memory_space=pl.ANY)
    item_grad, loss, query_grad = pl.pallas_call(
        functools.partial(item_grad_kernel, blocks),
        in_specs=[in_vmem] * (2 * blocks + 3) + [anywhere] * 2,
        out_specs=[in_vmem, anywhere, anywhere],
        out_shape=[
            struct((pairs, width), f32),
            struct((1, pairs), f32),
            struct((pairs, width), f32),
        ],
        scratch_shapes=[pltpu.SemaphoreType.DMA((2,))],
        compiler_params=params(12),
        name="item_grads",
    )(*queries, *items, own_sum, item_unit, item_scale, loss, query_grad)
    return loss.reshape(pairs), item_grad, query_grad


def solution(mesh):
    placed = (P("table", None), P(), P(), P(("blk", "table"), None), P(("blk", "table"), None))
    return jax.shard_map(
        local,
        mesh=mesh,
        in_specs=placed,
        out_specs=(P(("blk", "table")), P(("blk", "table"), None), P(("blk", "table"), None)),
        check_vma=False,
    )
```

```python
import functools

import jax
import jax.numpy as jnp
from jax import lax
from jax.experimental import pallas as pl
from jax.experimental.pallas import tpu as pltpu
from jax.sharding import PartitionSpec as P

EPS = 1e-06
INV_TEMP = 20.0


def params(mebibytes):
    return pltpu.CompilerParams(vmem_limit_bytes=mebibytes * 1024 * 1024)


def iota(shape, dim):
    return lax.broadcasted_iota(jnp.int32, shape, dim)


def row_dot(left, right):
    return lax.dot_general(
        left, right, (((1,), (1,)), ((), ())), preferred_element_type=jnp.float32
    )


def col_dot(left, right):
    return lax.dot_general(
        left, right, (((0,), (0,)), ((), ())), preferred_element_type=jnp.float32
    )


def dot(left, right):
    return jnp.dot(left, right, preferred_element_type=jnp.float32)


def unit_rows(vectors):
    scale = lax.rsqrt(jnp.sum(vectors * vectors, axis=-1, keepdims=True) + EPS)
    return vectors * scale, scale


def unit_backward(grad, unit, scale):
    return scale * (grad - unit * jnp.sum(unit * grad, axis=-1, keepdims=True))


def packed_lists(relative, rows_dev, askers, codes, chips, capacity):
    bags, pairs = codes[0].shape
    lists = len(askers) * chips
    place = lax.axis_index("table")
    half = 2 * chips
    list_of = iota((lists, pairs), 0)
    chip = relative(place % half // 2, list_of % chips)
    asker = list_of // chips
    core = place % 2
    for at, name in enumerate(askers):
        if name >= 4:
            core = jnp.where(asker == at, 1 - place % 2, core)
    start = (place // half * half + chip * 2 + core) * rows_dev
    named = jnp.zeros((lists, pairs), jnp.float32)
    rows = jnp.zeros((lists, pairs), jnp.int32)
    kind = jnp.zeros((lists, pairs), jnp.int32)
    for k in range(bags):
        code = codes[(0, 1, 2, 3, 0, 2)[askers[0]]][k : k + 1, :]
        for at, name in enumerate(askers[1:], 1):
            code = jnp.where(asker == at, codes[(0, 1, 2, 3, 0, 2)[name]][k : k + 1, :], code)
        row = code - start
        hit = (row >= 0) & (row < rows_dev)
        named = jnp.where(hit, 1.0, named)
        rows = jnp.where(hit, row, rows)
        kind = jnp.where(hit, 1 if k < bags // 2 else 2, kind)
    before = jnp.where(iota((pairs, pairs), 0) < iota((pairs, pairs), 1), 1.0, 0.0)
    slot = dot(named.astype(jnp.bfloat16), before.astype(jnp.bfloat16)).astype(jnp.int32)
    slot = jnp.where(named > 0.0, slot, -1)
    digits = [rows // 256, rows % 256, kind, iota((lists, pairs), 1)]
    packed = jnp.concatenate([d.astype(jnp.float32) for d in digits], axis=0).astype(jnp.bfloat16)
    places = iota((capacity, pairs), 0)
    for s in range(lists):
        chosen = jnp.where(slot[s : s + 1, :] == places, 1.0, 0.0).astype(jnp.bfloat16)
        got = row_dot(packed, chosen).astype(jnp.int32)
        high, low, which, pair = [got[i * lists + s : i * lists + s + 1, :] for i in range(4)]
        yield s // chips, s % chips, high * 256 + low, which, pair


def route_kernel(relative, rows_dev, *refs):
    codes, requests = refs[:4], refs[5:]
    capacity = requests[0].shape[1]
    lists = packed_lists(relative, rows_dev, (0, 1, 2, 3), codes, len(requests), capacity)
    for at, j, row, _, _ in lists:
        requests[j][at : at + 1, :] = 2 * row


def bag_kernel(relative, rows_dev, *refs):
    codes, outs = refs[:4], refs[4:]
    half, capacity = outs[0].shape
    pairs = codes[0].shape[1]
    chips = half // 2
    lists = packed_lists(relative, rows_dev, (0, 4, 2, 5), codes, chips, capacity)
    for at, j, _, which, pair in lists:
        place = at % 2 * chips + j
        outs[at // 2][place : place + 1, :] = (which - 1) * pairs + pair


def touch_kernel(table_hbm, out_ref, rows_ref, sem):
    copy = pltpu.make_async_copy(table_hbm.at[pl.ds(0, rows_ref.shape[0]), :], rows_ref, sem)
    copy.start()
    copy.wait()
    out_ref[...] = rows_ref[...].astype(jnp.float32)


def widen_kernel(table_ref, wide_ref):
    width = table_ref.shape[1]
    step = 128

    def widen(i, carry):
        start = pl.multiple_of(i * step, step)
        part = table_ref[pl.ds(start, step), :].astype(jnp.float32)
        wide_ref[pl.ds(2 * start, step, stride=2), :] = part[:, : width // 2]
        wide_ref[pl.ds(2 * start + 1, step, stride=2), :] = part[:, width // 2 :]
        return carry

    lax.fori_loop(0, table_ref.shape[0] // step, widen, 0)


def gather_kernel(chips, askers, *refs):
    wanted, wide_ref, refs = refs[:chips], refs[chips], refs[chips + 1 :]
    outs, (index_ref, stage, sems) = refs[: len(askers)], refs[len(askers) :]
    _, capacity, width = outs[0].shape
    group = 16
    copies = [
        pltpu.make_async_copy(wanted[chips - 1 - j], index_ref.at[j], sems.at[j])
        for j in range(chips)
    ]
    for copy in copies:
        copy.start()
    for copy in copies:
        copy.wait()
    for asker, out_ref in zip(askers, outs):
        for j in range(chips):
            for base in range(0, capacity, group):
                found = [
                    wide_ref[pl.ds(index_ref[j, asker, base + i], 2), :] for i in range(group)
                ]
                for i in range(group):
                    stage[pl.ds(2 * (base + i), 2), :] = found[i]
            for part in range(2):
                values = stage[pl.ds(part, capacity, stride=2), :]
                out_ref[j, :, part * (width // 2) : (part + 1) * (width // 2)] = values.astype(
                    jnp.bfloat16
                )


def pack_kernel(chips, same_ref, swapped_ref, *out_refs):
    for out_ref, j in zip(out_refs, range(chips - 1, 0, -1)):
        out_ref[0] = same_ref[j]
        out_ref[1] = swapped_ref[j]


def bag_sums(bag_ref, rows, bags, first):
    total = None
    for at, values in enumerate(rows):
        chosen = bag_ref[at : at + 1, :] == first + iota((bags, bag_ref.shape[1]), 0)
        part = dot(jnp.where(chosen, 1.0, 0.0).astype(jnp.bfloat16), values)
        total = part if total is None else total + part
    return total


def lists_of(order, same_ref, swapped_ref, message_refs):
    chips = len(order) + 1
    return [
        own_ref[0] if j == 0 else message_refs[order.index(j)][f]
        for f, own_ref in enumerate((same_ref, swapped_ref))
        for j in range(chips)
    ]


def sum_kernel(order, kind, bag_ref, same_ref, swapped_ref, *refs):
    out_ref = refs[-1]
    pairs = out_ref.shape[0]
    rows = lists_of(order, same_ref, swapped_ref, refs[:-1])
    out_ref[...] = bag_sums(bag_ref, rows, pairs, kind * pairs).astype(out_ref.dtype)


def item_kernel(order, bag_ref, far_ref, same_ref, swapped_ref, *refs):
    messages, (unit_ref, scale_ref, bf_ref) = refs[:-3], refs[-3:]
    pairs = bf_ref.shape[0]
    rows = lists_of(order, same_ref, swapped_ref, messages)
    total = bag_sums(bag_ref, rows, pairs, pairs) + far_ref[...].astype(jnp.float32)
    unit, scale = unit_rows(total)
    unit_ref[...] = unit
    scale_ref[...] = scale
    bf_ref[...] = unit.astype(jnp.bfloat16)


def tower_kernel(
    near_ref, far_ref, first_ref, second_ref, unit_ref, scale_ref, bf_ref, slope_ref
):
    query_in = (near_ref[...] + far_ref[...].astype(jnp.float32)).astype(jnp.bfloat16)
    query_in = (0.5 * query_in.astype(jnp.float32)).astype(jnp.bfloat16)
    step = 1024
    total = None
    for at in range(0, first_ref.shape[1], step):
        pre = dot(query_in, first_ref[:, at : at + step])
        turn = jnp.tanh(pre)
        hidden = pre + pre * turn
        turn = 0.5 * turn
        slope_ref[:, at : at + step] = (0.5 + turn) + hidden * (0.5 - turn)
        part = dot(hidden.astype(jnp.bfloat16), second_ref[at : at + step, :])
        total = part if total is None else total + part
    unit, scale = unit_rows(total)
    unit_ref[...] = unit
    scale_ref[...] = scale
    bf_ref[...] = unit.astype(jnp.bfloat16)


def group_exps(query, item):
    return jnp.exp(INV_TEMP * row_dot(query, item))


def row_sums(values):
    return jnp.sum(values, axis=1, keepdims=True)


def query_grad_kernel(blocks, *refs):
    query_ref, items, refs = refs[0], refs[1 : 1 + blocks], refs[1 + blocks :]
    first_ref, second_ref, slope_ref, unit_ref, scale_ref, loss_ref, grad_ref, item_sum_ref = refs
    query = query_ref[...]
    kept = [group_exps(query, item[...]) for item in items[:2]]
    total = sum(row_sums(exps) for exps in kept)
    for item in items[2:]:
        total = total + row_sums(group_exps(query, item[...]))
    inverse = 1.0 / total
    query_sum = jnp.zeros(query.shape, jnp.float32)
    for j, item in enumerate(items):
        exps = kept[j] if j < 2 else group_exps(query, item[...])
        probs = (exps * inverse).astype(jnp.bfloat16)
        query_sum = query_sum + dot(probs, item[...])
        if j == 0:
            item_sum_ref[...] = col_dot(probs, query)
    wide_item = items[0][...].astype(jnp.float32)
    own = INV_TEMP * row_sums(query.astype(jnp.float32) * wide_item)
    loss_ref[...] = (jnp.log(total) - own).T
    out_grad = unit_backward(
        INV_TEMP * (query_sum - wide_item), unit_ref[...], scale_ref[...]
    ).astype(jnp.bfloat16)
    step = 1024
    total = None
    for at in range(0, first_ref.shape[1], step):
        back = row_dot(out_grad, second_ref[at : at + step, :])
        hidden_grad = (back * slope_ref[:, at : at + step]).astype(jnp.bfloat16)
        part = row_dot(hidden_grad, first_ref[:, at : at + step])
        total = part if total is None else total + part
    grad_ref[...] = total


def item_grad_kernel(blocks, *refs):
    queries, items, refs = refs[:blocks], refs[blocks : 2 * blocks], refs[2 * blocks :]
    item_sum_ref, unit_ref, scale_ref, loss_ref, query_grad_ref, grad_ref, *outs, sems = refs
    copies = [
        pltpu.make_async_copy(given, out, sems.at[i])
        for i, (given, out) in enumerate(zip((loss_ref, query_grad_ref), outs))
    ]
    for copy in copies:
        copy.start()
    item_sum = item_sum_ref[...]
    for i in range(1, blocks):
        query = queries[i][...]
        own_exps = group_exps(query, items[0][...])
        total = row_sums(own_exps)
        for j in range(1, blocks):
            total = total + row_sums(group_exps(query, items[j][...]))
        item_sum = item_sum + col_dot((own_exps * (1.0 / total)).astype(jnp.bfloat16), query)
    grad_ref[...] = unit_backward(
        INV_TEMP * (item_sum - queries[0][...].astype(jnp.float32)), unit_ref[...], scale_ref[...]
    )
    for copy in copies:
        copy.wait()


def rotated(shard, axis, by):
    count = lax.axis_size(axis)
    return lax.ppermute(shard, axis, [(i, (i + by) % count) for i in range(count)])


def struct(shape, dtype):
    return jax.ShapeDtypeStruct(shape, dtype)


def local(id_table, w_first, w_second, owner_ids, row_ids):
    pairs, bags = owner_ids.shape
    shards = lax.axis_size("table")
    blocks = lax.axis_size("blk")
    width = id_table.shape[1]
    hidden_units = w_first.shape[1]
    capacity = min(pairs, 3 * pairs * bags // (2 * shards))
    bf, f32 = jnp.bfloat16, jnp.float32

    half = shards // 2
    chips = half // 2
    power = chips & (chips - 1) == 0

    def relative(chip, j):
        return chip ^ j if power else (chip + j) % chips

    def to_chip(values, j, flip=0):
        if j == 0 and flip == 0:
            return values
        route = [
            (t, t // half * half + relative(t % half // 2, j) * 2 + (t % 2 ^ flip))
            for t in range(shards)
        ]
        return lax.ppermute(values, "table", route)

    def to_mirror(values):
        return lax.ppermute(values, "table", [(t, (t + half) % shards) for t in range(shards)])

    code = owner_ids * id_table.shape[0] + row_ids
    mirror_code = to_mirror(code)
    codes = [code, to_chip(code, 0, 1), mirror_code, to_chip(mirror_code, 0, 1)]
    touched = pl.pallas_call(
        touch_kernel,
        in_specs=[pl.BlockSpec(memory_space=pl.ANY)],
        out_shape=struct((16, width), f32),
        scratch_shapes=[pltpu.VMEM((16, width), bf), pltpu.SemaphoreType.DMA(())],
        compiler_params=params(52),
        name="touch",
    )(id_table)
    wide = pl.pallas_call(
        widen_kernel,
        out_shape=struct((2 * id_table.shape[0], width // 2), f32),
        compiler_params=params(8),
        name="widen",
    )(id_table)
    codes = [c.T for c in codes]
    requests = pl.pallas_call(
        functools.partial(route_kernel, relative, id_table.shape[0]),
        out_shape=[struct((4, capacity), jnp.int32)] * chips,
        compiler_params=params(4),
        name="route",
    )(*codes, touched)
    *codes, _ = lax.optimization_barrier((*codes, requests[0]))
    near_bags, far_bags = pl.pallas_call(
        functools.partial(bag_kernel, relative, id_table.shape[0]),
        out_shape=[struct((half, capacity), jnp.int32)] * 2,
        compiler_params=params(4),
        name="bag_lists",
    )(*codes)
    wanted = [to_chip(requests[j], j) for j in reversed(range(chips))][::-1]

    wide, near_bags, far_bags = lax.optimization_barrier((wide, near_bags, far_bags))

    def gather(askers):
        return pl.pallas_call(
            functools.partial(gather_kernel, chips, askers),
            in_specs=[pl.BlockSpec(memory_space=pl.ANY)] * chips
            + [pl.BlockSpec(memory_space=pltpu.VMEM)],
            out_shape=[struct((chips, capacity, width), bf)] * len(askers),
            scratch_shapes=[
                pltpu.SMEM((chips, 4, capacity), jnp.int32),
                pltpu.VMEM((2 * capacity, width // 2), f32),
                pltpu.SemaphoreType.DMA((chips,)),
            ],
            compiler_params=params(8),
            name="gather",
        )(*wanted[::-1], wide)

    order = list(range(chips - 1, 0, -1))

    def answered(same, swapped, order):
        messages = pl.pallas_call(
            functools.partial(pack_kernel, chips),
            out_shape=[struct((2, capacity, width), bf)] * (chips - 1),
            compiler_params=params(8),
            name="pack",
        )(same, swapped)
        arrived = []
        for j in order:
            back = j if power else (chips - j) % chips
            arrived.append(to_chip(messages[chips - 1 - back], back))
        return (same, swapped, *arrived), messages

    far_other, near_other = [to_chip(rows, 0, 1) for rows in gather((3, 1))]
    (far_same,), (near_same,) = gather((2,)), gather((0,))
    far_rows, _ = answered(far_same, far_other, order)
    near_rows, near_messages = answered(near_same, near_other, order[::-1])
    far_bags, _ = lax.optimization_barrier((far_bags, near_messages[0]))

    def sums(order, kind, bags, rows, dtype):
        return pl.pallas_call(
            functools.partial(sum_kernel, order, kind),
            out_shape=struct((pairs, width), dtype),
            compiler_params=params(8),
            name="item_sums" if kind else "query_sums",
        )(bags, *rows)

    far_item = sums(order, 1, far_bags, far_rows, bf)
    far_bags, _ = lax.optimization_barrier((far_bags, far_item))
    far_query = to_mirror(sums(order, 0, far_bags, far_rows, bf))
    far_item = to_mirror(far_item)
    item_unit, item_scale, item_bf = pl.pallas_call(
        functools.partial(item_kernel, order[::-1]),
        out_shape=[
            struct((pairs, width), f32),
            struct((pairs, 1), f32),
            struct((pairs, width), bf),
        ],
        compiler_params=params(8),
        name="items",
    )(near_bags, far_item, *near_rows)
    near_bags, _ = lax.optimization_barrier((near_bags, item_bf))
    near_query = sums(order[::-1], 0, near_bags, near_rows, f32)
    items = [item_bf] + [rotated(item_bf, "blk", by) for by in range(1, blocks)]
    query_unit, query_scale, query_bf, slope = pl.pallas_call(
        tower_kernel,
        out_shape=[
            struct((pairs, width), f32),
            struct((pairs, 1), f32),
            struct((pairs, width), bf),
            struct((pairs, hidden_units), f32),
        ],
        compiler_params=params(12),
        name="tower",
    )(near_query, far_query, w_first, w_second)
    queries = [query_bf] + [rotated(query_bf, "blk", by) for by in range(1, blocks)]
    loss, query_grad, own_sum = pl.pallas_call(
        functools.partial(query_grad_kernel, blocks),
        out_shape=[
            struct((1, pairs), f32),
            struct((pairs, width), f32),
            struct((pairs, width), f32),
        ],
        compiler_params=params(12),
        name="query_grads",
    )(query_bf, *items, w_first, w_second, slope, query_unit, query_scale)
    queries, loss = lax.optimization_barrier((queries, loss))
    in_vmem, anywhere = pl.BlockSpec(memory_space=pltpu.VMEM), pl.BlockSpec(memory_space=pl.ANY)
    item_grad, loss, query_grad = pl.pallas_call(
        functools.partial(item_grad_kernel, blocks),
        in_specs=[in_vmem] * (2 * blocks + 3) + [anywhere] * 2,
        out_specs=[in_vmem, anywhere, anywhere],
        out_shape=[
            struct((pairs, width), f32),
            struct((1, pairs), f32),
            struct((pairs, width), f32),
        ],
        scratch_shapes=[pltpu.SemaphoreType.DMA((2,))],
        compiler_params=params(12),
        name="item_grads",
    )(*queries, *items, own_sum, item_unit, item_scale, loss, query_grad)
    return loss.reshape(pairs), item_grad, query_grad


def solution(mesh):
    placed = (P("table", None), P(), P(), P(("blk", "table"), None), P(("blk", "table"), None))
    return jax.shard_map(
        local,
        mesh=mesh,
        in_specs=placed,
        out_specs=(P(("blk", "table")), P(("blk", "table"), None), P(("blk", "table"), None)),
        check_vma=False,
    )
```
